32 devices in a mesh: groups: 2 (over x), ctx: 16 (over z, y, core).
Axes of the slice: x: 2, y: 2, z: 4, core: 2. Of those that a mesh axis runs over, the one named last changes fastest.
Arguments:
- query_gate: bfloat16 [4096, 4096], P(('groups', 'ctx')), parts along dimension 0, may hold values from -6 to 6
- key_branch: bfloat16 [4096, 4096], P(('groups', 'ctx')), parts along dimension 0, may hold values from -6 to 6
- value_branch: bfloat16 [4096, 4096], P(('groups', 'ctx')), parts along dimension 0, may hold values from -6 to 6
- out_grad: bfloat16 [4096, 4096], P(('groups', 'ctx')), parts along dimension 0, may hold values from -6 to 6
- filter_taps: bfloat16 [4096, 256], P('ctx'), may hold values from -0.375 to 0.375
- doc_blocks: int32 [8], P('groups'), parts along dimension 0, may hold values from 1 to 8, 16 in all
Outputs:
- key_grad: bfloat16 [4096, 4096], P(('groups', 'ctx')), parts along dimension 0
- value_grad: bfloat16 [4096, 4096], P(('groups', 'ctx')), parts along dimension 0
- filter_grad: float32 [8192, 256], P(('groups', 'ctx')), parts along dimension 0
The draws below stay inside these ranges and needn't reach their ends.
There are 2 independent parts, one for each index of `groups`. The reference program is written for one: setup_inputs(seed, part) draws one part's arguments, and reference() takes and returns one part's arrays. A program takes and returns all parts, laid end to end along the dimension named above; an argument that names none is the same for every part. Nothing has to cross between parts.
Inputs may be any that keep to these rules, and one draw needn't show every extreme that they name: `doc_blocks`: documents follow one another along the sequence, each a whole number of blocks of 128 tokens; the lengths sum to 16 and the longest is exactly 8 blocks.
All inputs are finite; a program needn't handle non-finite values.
Results may differ from the reference program's by a relative error of at most 0.005.
Values may be sent and summed in bfloat16 or wider, within the bound.
No kernel may reach another device: no remote copies, remote signals or barrier semaphores. Data moves between devices by JAX's collectives and lax.ppermute only.
A program may use at most 128 MiB of HBM per device.

```python
import math
import jax
import jax.numpy as jnp
import numpy as np
from jax import lax

D = 4096
TOK_DEV = 128
REACH = 2
DOC_MOST = 8
BLOCKS = 16
TAPS = 256
DOCS = 4
TOKENS = 2048


def shard_levels(rng, shape, cuts, smallest, largest):
    loudness = 1.0
    for dim, parts in cuts:
        steps = jax.random.uniform(jax.random.fold_in(jax.random.fold_in(rng, 6), dim), (parts,), jnp.float32, smallest / len(cuts), largest / len(cuts))
        loudness = loudness * jnp.repeat(jnp.exp(steps), shape[dim] // parts).reshape((-1,) + (1,) * (len(shape) - 1 - dim))
    return loudness


def length_profile(number_of, total, most, slope):
    weights = [(1 << 20) // math.isqrt(standing ** slope) + 1 for standing in range(2, number_of + 1)]
    rest, holding = total - most - (number_of - 1), [1] * (number_of - 1)
    while rest > 0:
        free = [i for i in range(number_of - 1) if holding[i] < most]
        mass, remaining = sum([weights[i] for i in free]), rest
        for i in free:
            extra = min(most - holding[i], max(1, remaining * weights[i] // mass), rest)
            holding[i] = holding[i] + extra
            rest = rest - extra
    return np.array([most] + holding)


def uneven_parts(rng, count, total, bound, lean):
    if count == 2:
        one = jax.random.randint(rng, (), max(1, total - bound), min(bound, total - 1) + 1)
        return jnp.stack([one, total - one])
    sizes = jnp.asarray(length_profile(count, total, bound, lean), jnp.int32)
    pairs = (count - 1) // 2
    giver, receiver = sizes[1:1 + 2 * pairs:2], sizes[2:2 + 2 * pairs:2]
    room = jnp.minimum(giver - 1, bound - receiver)
    moved = jax.random.randint(jax.random.fold_in(rng, 1), (pairs,), 0, 1 << 20) % (room + 1)
    sizes = sizes.at[1:1 + 2 * pairs:2].set(giver - moved).at[2:2 + 2 * pairs:2].set(receiver + moved)
    return sizes[jax.random.permutation(jax.random.fold_in(rng, 2), count)]


def normal_values(stream_key, shape, deviation, limit, shards=(), kind=jnp.bfloat16):
    entries = deviation * jax.random.normal(stream_key, shape, jnp.float32)
    if shards:
        entries = entries * shard_levels(stream_key, shape, shards, -0.22, 0.18)
    return jnp.clip(entries, -limit, limit).astype(kind)


def setup_inputs(seed: int = 0, part: int = 0) -> dict:
    splits = jax.random.split(jax.random.key(seed), 7)
    own_keys = jax.random.split(jax.random.fold_in(splits[6], part), 7)
    query_gate = normal_values(own_keys[0], (TOKENS, D), 1.0, 6.0, ((0, 16),))
    key_branch = normal_values(own_keys[1], (TOKENS, D), 1.0, 6.0, ((0, 16),))
    value_branch = normal_values(own_keys[2], (TOKENS, D), 1.0, 6.0, ((0, 16),))
    out_grad = normal_values(own_keys[3], (TOKENS, D), 1.0, 6.0, ((0, 16),))
    filter_taps = normal_values(splits[4], (D, TAPS), TAPS ** -0.5, 0.375, ((0, 16),))
    doc_blocks = uneven_parts(own_keys[5], DOCS, BLOCKS, DOC_MOST, 1).astype(jnp.int32)
    return {"query_gate": query_gate, "key_branch": key_branch, "value_branch": value_branch, "out_grad": out_grad, "filter_taps": filter_taps, "doc_blocks": doc_blocks}


def block_documents(doc_blocks):
    doc_starts = jnp.cumsum(doc_blocks) - doc_blocks
    block_ids = jnp.arange(BLOCKS, dtype=jnp.int32)
    return lax.optimization_barrier(jnp.sum((doc_starts[None, :] <= block_ids[:, None]).astype(jnp.int32), axis=1)) - 1

def live_pairs(doc_blocks):
    owners = block_documents(doc_blocks)
    block_ids = jnp.arange(BLOCKS, dtype=jnp.int32)
    pair_masks = []
    for offset in range(REACH + 1):
        partner = jnp.minimum(block_ids + offset, BLOCKS - 1).astype(jnp.int32)
        inside = block_ids + offset < BLOCKS
        pair_masks.append(jnp.where(inside & (owners[partner] == owners), 1.0, 0.0).astype(jnp.float32))
    return jnp.stack(pair_masks, axis=0)

def reference(query_gate, key_branch, value_branch, out_grad, filter_taps, doc_blocks):
    group_width = 256 if D % 256 == 0 else D
    groups = D // group_width
    length = 2 * TOK_DEV
    conv_input = (key_branch.astype(jnp.float32) * value_branch.astype(jnp.float32)).astype(jnp.bfloat16)
    gated_grad = (out_grad.astype(jnp.float32) * query_gate.astype(jnp.float32)).astype(jnp.bfloat16)
    pair_masks = live_pairs(doc_blocks)

    def by_group(array):
        return array.reshape(BLOCKS, TOK_DEV, groups, group_width).transpose(2, 0, 1, 3)

    def one_group(pieces):
        conv_part, grad_part, taps_part = pieces
        conv_spec = jnp.fft.rfft(conv_part.astype(jnp.float32), n=length, axis=1)
        padded = jnp.concatenate([grad_part.astype(jnp.float32), jnp.zeros((REACH, TOK_DEV, group_width), jnp.float32)], axis=0)
        lag_taps = jnp.concatenate([jnp.zeros((TOK_DEV, group_width), jnp.float32), taps_part.astype(jnp.float32).T, jnp.zeros((TOK_DEV, group_width), jnp.float32)], axis=0)
        grad_spec = jnp.zeros(conv_spec.shape, conv_spec.dtype)
        lag_grad = jnp.zeros((TAPS + 2 * TOK_DEV, group_width), jnp.float32)
        for offset in range(REACH + 1):
            lag_start = offset * TOK_DEV
            window = jnp.concatenate([lag_taps[lag_start + TOK_DEV:lag_start + 2 * TOK_DEV], lag_taps[lag_start:lag_start + TOK_DEV]], axis=0)
            window_spec = jnp.fft.rfft(window, n=length, axis=0)
            later_spec = jnp.fft.rfft(padded[offset:offset + BLOCKS], n=length, axis=1) * pair_masks[offset][:, None, None]
            grad_spec = grad_spec + later_spec * jnp.conj(window_spec)[None]
            cross_corr = jnp.fft.irfft(lax.optimization_barrier(jnp.sum(later_spec * jnp.conj(conv_spec), axis=0)), n=length, axis=0)
            lag_grad = lag_grad.at[lag_start + TOK_DEV:lag_start + 2 * TOK_DEV].add(cross_corr[:TOK_DEV])
            lag_grad = lag_grad.at[lag_start:lag_start + TOK_DEV].add(cross_corr[TOK_DEV:])
        grad_input = jnp.fft.irfft(grad_spec, n=length, axis=1)[:, :TOK_DEV]
        return (grad_input, lag_grad[TOK_DEV:TOK_DEV + TAPS].T)
    grad_blocks, tap_grads = lax.map(one_group, (by_group(conv_input), by_group(gated_grad), filter_taps.reshape(groups, group_width, TAPS)))
    grad_input = grad_blocks.transpose(1, 2, 0, 3).reshape(TOKENS, D)
    norm_scale = 1.0 / math.sqrt(TOKENS)
    key_grad = (grad_input * value_branch.astype(jnp.float32)).astype(jnp.bfloat16)
    value_grad = (grad_input * key_branch.astype(jnp.float32)).astype(jnp.bfloat16)
    filter_grad = tap_grads.reshape(D, TAPS) * norm_scale
    return (key_grad, value_grad, filter_grad)
```

```python
import math
from functools import partial

import jax
import jax.numpy as jnp
import ml_dtypes
import numpy as np
from jax import lax
from jax.experimental import pallas as pl
from jax.experimental.pallas import tpu as pltpu
from jax.sharding import PartitionSpec as P

QUAD = 4
CHUNKS = 2
REACH = 2
TILE = 256
F32 = jnp.float32
BF16 = jnp.bfloat16
SMEM = pl.BlockSpec(memory_space=pltpu.SMEM)
VMEM = pl.BlockSpec(memory_space=pltpu.VMEM)
PARAMS = pltpu.CompilerParams(vmem_limit_bytes=40 * 1024 * 1024)


def split_bf16(table):
    high = table.astype(ml_dtypes.bfloat16)
    low = (table - high.astype(np.float64)).astype(ml_dtypes.bfloat16)
    return high, low


def tables(rows):
    length = 2 * rows
    omega = 2.0 * math.pi * (np.arange(rows) + 0.5) / length
    angle = omega[:, None] * np.arange(length)[None, :]
    forward = np.concatenate([np.cos(angle), -np.sin(angle)], axis=0)
    high, low = split_bf16(forward)
    half = np.concatenate([high[:, :rows], low[:, :rows]], axis=1)
    back_high, back_low = split_bf16(forward[:, :rows].T / rows)
    back = np.concatenate([back_high, back_low], axis=0)
    return np.concatenate([high, low, half, back], axis=0)


def dot(left, right):
    return jnp.dot(left, right, preferred_element_type=F32)


def conj_product(left, right):
    (lr, li), (rr, ri) = left, right
    return lr * rr + li * ri, li * rr - lr * ri


def halves(spectrum):
    rows = spectrum.shape[0] // 2
    return spectrum[:rows], spectrum[rows:]


def add(left, right):
    return left[0] + right[0], left[1] + right[1]


def invert(back, real, imag):
    rows = real.shape[0]
    spectrum = jnp.concatenate([real, imag], axis=0)
    high = spectrum.astype(BF16)
    low = (spectrum - high.astype(F32)).astype(BF16)
    both = dot(back, high)
    return both[:rows] + both[rows:] + dot(back[:rows], low)


def prep_kernel(pieces, offset, pos_ref, left_ref, right_ref, *outs):
    place = pos_ref[0] % QUAD
    count, width = pieces
    for k, out in enumerate(outs):
        member = lax.bitwise_xor(place, k)
        for i in range(count):
            lanes = pl.ds(pl.multiple_of(offset(i, member), 128), width)
            product = left_ref[:, lanes].astype(F32) * right_ref[:, lanes].astype(F32)
            out[:, i * width : (i + 1) * width] = product.astype(BF16)


def halo_kernel(pos_ref, *refs):
    place = pos_ref[0] % QUAD
    out = refs[-1]
    rows = refs[0].shape[0]
    for block in range(REACH):
        for k in range(QUAD):

            @pl.when(lax.bitwise_xor(place, k) == block)
            def _():
                out[block * rows : (block + 1) * rows, :] = refs[k][...]


def conv_kernel(chunk, quads, docs, pos_ref, docs_ref, table_ref, halo_ref, *refs):
    grads, inputs, taps = refs[:QUAD], refs[QUAD : 2 * QUAD], refs[2 * QUAD : 2 * QUAD + quads]
    outs = refs[2 * QUAD + quads : 3 * QUAD + quads]
    terms = refs[3 * QUAD + quads : 3 * QUAD + 2 * quads]
    grad_all, input_all, taps_all, out_all, terms_all = refs[3 * QUAD + 2 * quads :]
    rows, width = grads[0].shape
    length = 2 * rows
    piece = taps[0].shape[0] // CHUNKS
    place, quad = pos_ref[0] % QUAD, pos_ref[0] // QUAD
    joined = []
    for j in range(QUAD + 1):
        same, end = jnp.int32(1), jnp.int32(0)
        for d in range(docs):
            end = end + docs_ref[d]
            same = jnp.where(end == quad * QUAD + j + 1, 0, same)
        joined.append(same.astype(F32))
    for k in range(QUAD):
        at = pl.ds(pl.multiple_of(lax.bitwise_xor(place, k) * rows, rows), rows)
        grad_all[at, :] = grads[k][...]
        input_all[at, :] = inputs[k][...]
    grad_all[QUAD * rows :, :] = halo_ref[...]
    for s in range(quads):
        at = pl.ds(pl.multiple_of((quad + s) % quads * piece, piece), piece)
        taps_all[at, :] = taps[s][chunk * piece : (chunk + 1) * piece, :]
    high, low = table_ref[:length], table_ref[length : 2 * length]
    half, back = table_ref[2 * length : 3 * length], table_ref[3 * length :]
    for first in range(0, width, TILE):
        lanes = slice(first, min(first + TILE, width))
        filters = []
        for segment in range(REACH):
            part = taps_all[lanes, segment * rows : (segment + 1) * rows]
            twice = jnp.concatenate([part, part], axis=1)
            filters.append(
                halves(lax.dot_general(half, twice, (((1,), (1,)), ((), ())), preferred_element_type=F32))
            )
        windows = []
        for j in range(QUAD + 1):
            ahead = grad_all[(j + 1) * rows : (j + 2) * rows, lanes].astype(F32) * joined[j]
            window = jnp.concatenate([grad_all[j * rows : (j + 1) * rows, lanes], ahead.astype(BF16)], axis=0)
            windows.append(dot(high, window) + dot(low, window))
        sums = [None] * REACH
        for j in range(QUAD):
            held = input_all[j * rows : (j + 1) * rows, lanes]
            source = halves(dot(half, jnp.concatenate([held, held], axis=0)))
            near, far = halves(windows[j]), halves(windows[j + 1] * joined[j])
            real, imag = add(conj_product(near, filters[0]), conj_product(far, filters[1]))
            out_all[j * rows : (j + 1) * rows, lanes] = invert(back, real, imag).astype(BF16)
            for segment, window in enumerate((near, far)):
                term = conj_product(window, source)
                sums[segment] = term if j == 0 else add(sums[segment], term)
        for segment in range(REACH):
            lags = invert(back, *sums[segment])
            terms_all[lanes, segment * rows : (segment + 1) * rows] = lags.T
    for k in range(QUAD):
        at = pl.ds(pl.multiple_of(lax.bitwise_xor(place, k) * rows, rows), rows)
        outs[k][...] = out_all[at, :]
    for s in range(quads):
        at = pl.ds(pl.multiple_of((quad + s) % quads * piece, piece), piece)
        terms[s][...] = terms_all[at, :].astype(terms[s].dtype)


def final_kernel(pieces, offsets, pos_ref, key_ref, value_ref, *refs):
    grads, (key_out, value_out) = refs[:-2], refs[-2:]
    place = pos_ref[0] % QUAD
    count, width = pieces
    for chunk in range(CHUNKS):
        for k in range(QUAD):
            member = lax.bitwise_xor(place, k)
            for i in range(count):
                lanes = pl.ds(pl.multiple_of(offsets[chunk](i, member), 128), width)
                grad = grads[chunk * QUAD + k][:, i * width : (i + 1) * width].astype(F32)
                key_out[:, lanes] = (grad * value_ref[:, lanes].astype(F32)).astype(BF16)
                value_out[:, lanes] = (grad * key_ref[:, lanes].astype(F32)).astype(BF16)


def shards(query_gate, key_branch, value_branch, out_grad, filter_taps, doc_blocks):
    blocks = lax.axis_size("ctx")
    quads = blocks // QUAD
    rows, channels = query_gate.shape
    lags = filter_taps.shape[1]
    piece = channels // (QUAD * quads * CHUNKS)
    width = quads * piece
    pos = lax.axis_index("ctx").astype(jnp.int32).reshape(1)
    table = jnp.asarray(tables(rows))
    aligned = piece % 128 == 0

    def grouped(array):
        if aligned:
            return array
        parts = array.reshape(rows, quads, QUAD, CHUNKS, piece)
        return parts.transpose(0, 2, 3, 1, 4).reshape(rows, channels)

    def ungrouped(array):
        if aligned:
            return array
        parts = array.reshape(rows, QUAD, CHUNKS, quads, piece)
        return parts.transpose(0, 3, 1, 2, 4).reshape(rows, channels)

    if aligned:
        pieces = (quads, piece)
        offsets = [lambda i, member, c=c: ((i * QUAD + member) * CHUNKS + c) * piece for c in range(CHUNKS)]
    else:
        pieces = (1, width)
        offsets = [lambda i, member, c=c: (member * CHUNKS + c) * width for c in range(CHUNKS)]

    def to_member(value, k):
        if k == 0:
            return value
        return lax.ppermute(value, "ctx", [(i, i ^ k) for i in range(blocks)])

    def to_quad(value, s):
        if s == 0:
            return value
        return lax.ppermute(value, "ctx", [(i, (i + QUAD * s) % blocks) for i in range(blocks)])

    key_branch, value_branch = grouped(key_branch), grouped(value_branch)
    out_grad, query_gate = grouped(out_grad), grouped(query_gate)
    taps = [to_quad(filter_taps, quads - s if s else 0) for s in range(quads)]

    block_type = jax.ShapeDtypeStruct((rows, width), BF16)

    def prep(chunk, left, right, name):
        sent = pl.pallas_call(
            partial(prep_kernel, pieces, offsets[chunk]),
            out_shape=[block_type] * QUAD,
            in_specs=[SMEM, VMEM, VMEM],
            out_specs=[VMEM] * QUAD,
            compiler_params=PARAMS,
            name=name,
        )(pos, left, right)
        return [to_member(sent[k], k) for k in range(QUAD)]

    grads, inputs, halos = [], [], []
    for chunk in range(CHUNKS):
        grads.append(prep(chunk, out_grad, query_gate, f"gated_grad_{chunk}"))
        inputs.append(prep(chunk, key_branch, value_branch, f"conv_input_{chunk}"))
    results, terms = [], []
    for chunk in range(CHUNKS):
        first_blocks = pl.pallas_call(
            halo_kernel,
            out_shape=jax.ShapeDtypeStruct((REACH * rows, width), BF16),
            in_specs=[SMEM] + [VMEM] * QUAD,
            out_specs=VMEM,
            compiler_params=PARAMS,
            name=f"halo_{chunk}",
        )(pos, *grads[chunk])
        halo = lax.ppermute(first_blocks, "ctx", [(i, i - QUAD) for i in range(QUAD, blocks)])
        done = pl.pallas_call(
            partial(conv_kernel, chunk, quads, doc_blocks.shape[0]),
            out_shape=[block_type] * QUAD
            + [jax.ShapeDtypeStruct((piece, lags), BF16 if s else F32) for s in range(quads)],
            in_specs=[SMEM, SMEM, VMEM, VMEM] + [VMEM] * (2 * QUAD + quads),
            out_specs=[VMEM] * (QUAD + quads),
            scratch_shapes=[
                pltpu.VMEM(((QUAD + REACH) * rows, width), BF16),
                pltpu.VMEM((QUAD * rows, width), BF16),
                pltpu.VMEM((width, lags), BF16),
                pltpu.VMEM((QUAD * rows, width), BF16),
                pltpu.VMEM((width, lags), F32),
            ],
            compiler_params=PARAMS,
            name=f"conv_{chunk}",
        )(pos, doc_blocks, table, halo, *grads[chunk], *inputs[chunk], *taps)
        results.extend(to_member(done[k], k) for k in range(QUAD))
        received = [to_quad(done[QUAD + s], s) for s in range(quads)]
        total = received[0]
        for term in received[1:]:
            total = total + term.astype(F32)
        terms.append(total)
    filter_grad = jnp.concatenate(terms, axis=0) * (1.0 / math.sqrt(rows * blocks))
    step = 32
    key_grad, value_grad = pl.pallas_call(
        partial(final_kernel, pieces, offsets),
        grid=(rows // step,),
        out_shape=[jax.ShapeDtypeStruct((rows, channels), BF16)] * 2,
        in_specs=[SMEM]
        + [pl.BlockSpec((step, channels), lambda i: (i, 0))] * 2
        + [pl.BlockSpec((step, width), lambda i: (i, 0))] * (CHUNKS * QUAD),
        out_specs=[pl.BlockSpec((step, channels), lambda i: (i, 0))] * 2,
        compiler_params=PARAMS,
        name="gate_products",
    )(pos, key_branch, value_branch, *results)
    return (ungrouped(key_grad), ungrouped(value_grad), filter_grad)


def solution(mesh):
    in_specs = (
        P(("groups", "ctx"), None),
        P(("groups", "ctx"), None),
        P(("groups", "ctx"), None),
        P(("groups", "ctx"), None),
        P("ctx", None),
        P("groups"),
    )
    out_specs = (P(("groups", "ctx"), None), P(("groups", "ctx"), None), P(("groups", "ctx"), None))
    return jax.shard_map(shards, mesh=mesh, in_specs=in_specs, out_specs=out_specs, check_vma=False)
```

```python
import math
from functools import partial

import jax
import jax.numpy as jnp
import ml_dtypes
import numpy as np
from jax import lax
from jax.experimental import pallas as pl
from jax.experimental.pallas import tpu as pltpu
from jax.sharding import PartitionSpec as P

QUAD = 4
CHUNKS = 2
REACH = 2
TILE = 256
F32 = jnp.float32
BF16 = jnp.bfloat16
SMEM = pl.BlockSpec(memory_space=pltpu.SMEM)
VMEM = pl.BlockSpec(memory_space=pltpu.VMEM)
HBM = pl.BlockSpec(memory_space=pltpu.HBM)
ANY = pl.BlockSpec(memory_space=pl.ANY)
PARAMS = pltpu.CompilerParams(vmem_limit_bytes=40 * 1024 * 1024)


def halving_order(count):
    order = [0]
    while len(order) < count:
        order = [2 * n for n in order] + [2 * n + 1 for n in order]
    return order


def split_bf16(table):
    high = table.astype(ml_dtypes.bfloat16)
    low = (table - high.astype(np.float64)).astype(ml_dtypes.bfloat16)
    return high, low


def tables(rows):
    length = 2 * rows
    omega = 2.0 * math.pi * (np.arange(rows) + 0.5) / length
    angle = omega[:, None] * np.arange(length)[None, :]
    forward = np.concatenate([np.cos(angle), -np.sin(angle)], axis=0)
    high, low = split_bf16(forward)
    half = np.concatenate([high[:, :rows], low[:, :rows]], axis=1)
    back_high, back_low = split_bf16(forward[:, :rows].T / rows)
    back = np.concatenate([back_high, back_low], axis=0)
    return np.concatenate([high, low, half, back], axis=0)


def dot(left, right):
    return jnp.dot(left, right, preferred_element_type=F32)


def conj_product(left, right):
    (lr, li), (rr, ri) = left, right
    return lr * rr + li * ri, li * rr - lr * ri


def halves(spectrum):
    rows = spectrum.shape[0] // 2
    return spectrum[:rows], spectrum[rows:]


def add(left, right):
    return left[0] + right[0], left[1] + right[1]


def invert(back, real, imag):
    rows = real.shape[0]
    spectrum = jnp.concatenate([real, imag], axis=0)
    high = spectrum.astype(BF16)
    low = (spectrum - high.astype(F32)).astype(BF16)
    both = dot(back, high)
    return both[:rows] + both[rows:] + dot(back[:rows], low)


def cut_products(pieces, offset, sources, held, sems, outs):
    count, width = pieces
    section = held[0].shape[1] // count
    copies = []
    for i in range(count):
        lanes = pl.ds(i * section, section)
        for n, (source, target) in enumerate(zip(sources, held)):
            copies.append(pltpu.make_async_copy(source.at[:, lanes], target.at[:, lanes], sems.at[n, i]))
            copies[-1].start()
    for i in range(count):
        copies[2 * i].wait()
        copies[2 * i + 1].wait()
        for out, side, pair, chunks in outs:
            for n, chunk in enumerate(chunks):
                lanes = pl.ds(pl.multiple_of(offset(chunk, i, pair, side), 128), width)
                first = (n * count + i) * width
                out[:, first : first + width] = held[0][:, lanes] * held[1][:, lanes]


def grad_kernel(pieces, offset, pos_ref, left_hbm, right_hbm, own, near, same, other, left_ref, right_ref, sems):
    place = pos_ref[0] % QUAD
    core, chip = place % 2, place // 2
    every = range(CHUNKS)
    outs = [(same, core, 1 - chip, every), (other, 1 - core, 1 - chip, every)]
    outs += [(near, 1 - core, chip, every), (own, core, chip, every)]
    cut_products(pieces, offset, (left_hbm, right_hbm), (left_ref, right_ref), sems, outs)


def input_kernel(pieces, offset, pos_ref, left_hbm, right_hbm, own, near, *refs):
    far, (left_ref, right_ref, sems) = refs[:-3], refs[-3:]
    rows = own.shape[0]
    place = pos_ref[0] % QUAD
    core, chip = place % 2, place // 2
    outs = [(near, 1 - core, chip, range(CHUNKS)), (own, core, chip, range(CHUNKS))]
    for chunk, out in enumerate(far):
        outs += [(out.at[:rows, :], core, 1 - chip, [chunk]), (out.at[rows:, :], 1 - core, 1 - chip, [chunk])]
    cut_products(pieces, offset, (left_hbm, right_hbm), (left_ref, right_ref), sems, outs)


def pack_kernel(near_ref, came_ref, _, out):
    rows = near_ref.shape[0]
    out[:rows, :] = near_ref[...]
    out[rows:, :] = came_ref[rows:, :]


def filter_kernel(quads, pos_ref, table_ref, *refs):
    parts, out, taps_all = refs[:-2], refs[-2], refs[-1]
    quad = pos_ref[0] // QUAD
    channels, lags = taps_all.shape
    rows = lags // REACH
    half = table_ref[2 * lags : 3 * lags]
    width = channels // CHUNKS
    piece = width // quads
    held = [(part, at) for part in parts for at in range(0, part.shape[0], CHUNKS * piece)]
    for s, (part, first) in zip(halving_order(quads), held):
        for chunk in range(CHUNKS):
            at = pl.ds(pl.multiple_of(chunk * width + lax.bitwise_xor(quad, s) * piece, piece), piece)
            taps_all[at, :] = part[first + chunk * piece : first + (chunk + 1) * piece, :]
    for first in range(0, channels, TILE):
        for segment in range(REACH):
            taps = taps_all[first : first + TILE, segment * rows : (segment + 1) * rows]
            twice = jnp.concatenate([taps, taps], axis=1)
            spectrum = lax.dot_general(half, twice, (((1,), (1,)), ((), ())), preferred_element_type=F32)
            out[segment * lags : (segment + 1) * lags, first : first + TILE] = spectrum


def gate_kernel(*refs):
    del refs


def halo_kernel(chunks, pos_ref, *refs):
    place = pos_ref[0] % QUAD
    held, outs = refs[:QUAD], refs[-chunks:]
    rows, width = held[0].shape[0], outs[0].shape[1]
    for block in range(REACH):
        for k in range(QUAD):

            @pl.when(lax.bitwise_xor(place, k) == block)
            def _():
                for chunk, out in enumerate(outs):
                    out[block * rows : (block + 1) * rows, :] = held[k][:rows, chunk * width : (chunk + 1) * width]


def conv_kernel(chunk, quads, docs, pos_ref, docs_ref, table_ref, halo_ref, filter_ref, *refs):
    grads, (own_ref, far_ref, came_ref) = refs[:QUAD], refs[QUAD : QUAD + 3]
    outs, terms = refs[-6 - QUAD : -6], refs[-6:-4]
    grad_all, input_all, out_all, terms_all = refs[-4:]
    rows, width = grads[0].shape
    length = 2 * rows
    piece = width // quads
    place, quad = pos_ref[0] % QUAD, pos_ref[0] // QUAD
    joined = []
    for j in range(QUAD + 1):
        same, end = jnp.int32(1), jnp.int32(0)
        for d in range(docs):
            end = end + docs_ref[d]
            same = jnp.where(end == quad * QUAD + j + 1, 0, same)
        joined.append(same.astype(F32))
    for k in range(QUAD):
        at = pl.ds(pl.multiple_of(lax.bitwise_xor(place, k) * rows, rows), rows)
        grad_all[at, :] = grads[k][...]
        held = (own_ref, came_ref, far_ref, came_ref)[k]
        input_all[at, :] = held[(k // 3) * rows : (k // 3 + 1) * rows, :]
    grad_all[QUAD * rows :, :] = halo_ref[...]
    high, low = table_ref[:length], table_ref[length : 2 * length]
    half, back = table_ref[2 * length : 3 * length], table_ref[3 * length :]
    for first in range(0, width, TILE):
        lanes = slice(first, min(first + TILE, width))
        filters = [halves(filter_ref[n * length : (n + 1) * length, lanes]) for n in range(REACH)]
        windows = []
        for j in range(QUAD + 1):
            ahead = grad_all[(j + 1) * rows : (j + 2) * rows, lanes].astype(F32) * joined[j]
            window = jnp.concatenate([grad_all[j * rows : (j + 1) * rows, lanes], ahead.astype(BF16)], axis=0)
            windows.append(dot(high, window) + dot(low, window))
        sums = [None] * REACH
        for j in range(QUAD):
            held = input_all[j * rows : (j + 1) * rows, lanes]
            source = halves(dot(half, jnp.concatenate([held, held], axis=0)))
            near, far = halves(windows[j]), halves(windows[j + 1] * joined[j])
            real, imag = add(conj_product(near, filters[0]), conj_product(far, filters[1]))
            out_all[j * rows : (j + 1) * rows, lanes] = invert(back, real, imag).astype(BF16)
            for segment, window in enumerate((near, far)):
                term = conj_product(window, source)
                sums[segment] = term if j == 0 else add(sums[segment], term)
        for segment in range(REACH):
            lags = invert(back, *sums[segment])
            terms_all[lanes, segment * rows : (segment + 1) * rows] = lags.T
    for k in range(QUAD):
        at = pl.ds(pl.multiple_of(lax.bitwise_xor(place, k) * rows, rows), rows)
        outs[k][...] = out_all[at, :]
    for n, s in enumerate(halving_order(quads)):
        at = pl.ds(pl.multiple_of(lax.bitwise_xor(quad, s) * piece, piece), piece)
        sent, n = divmod(n, quads // 2)
        terms[sent][n * piece : (n + 1) * piece, :] = terms_all[at, :].astype(terms[sent].dtype)


def fold_kernel(kept_ref, came_ref, *refs):
    keep_ref, send_ref = refs[-2:]
    half = keep_ref.shape[0]
    keep_ref[...] = kept_ref[:half, :] + came_ref[:half, :].astype(F32)
    send_ref[...] = (kept_ref[half:, :] + came_ref[half:, :].astype(F32)).astype(BF16)


def final_kernel(chunk, pieces, offset, scale, terms, pos_ref, key_ref, value_ref, *refs):
    grads, filters = refs[:QUAD], refs[QUAD : QUAD + terms]
    filter_all, filter_sem, key_all, value_all, sems = refs[-5:]
    key_out, value_out, *filter_out = refs[-8 if terms else -7 : -5]
    place = pos_ref[0] % QUAD
    count, width = pieces
    copies = []
    for n in range(terms // 2):
        kept, came = filters[2 * n], filters[2 * n + 1]
        rows = kept.shape[0]
        filter_all[n * rows : (n + 1) * rows, :] = (kept[...] + came[...].astype(F32)) * scale
    for out in filter_out:
        copies.append(pltpu.make_async_copy(filter_all, out, filter_sem))
        copies[-1].start()
    for k in range(QUAD):
        member = lax.bitwise_xor(place, k)
        for i in range(count):
            n = k * count + i
            lanes = pl.ds(pl.multiple_of(offset(chunk, i, member // 2, member % 2), 128), width)
            held = slice(n * width, (n + 1) * width)
            grad = grads[k][:, i * width : (i + 1) * width]
            key_all[:, held] = grad * value_ref[:, lanes]
            value_all[:, held] = grad * key_ref[:, lanes]
            copies.append(pltpu.make_async_copy(key_all.at[:, held], key_out.at[:, lanes], sems.at[0, n]))
            copies.append(pltpu.make_async_copy(value_all.at[:, held], value_out.at[:, lanes], sems.at[1, n]))
            copies[-2].start()
            copies[-1].start()
    for copy in copies:
        copy.wait()


def shards(query_gate, key_branch, value_branch, out_grad, filter_taps, doc_blocks):
    blocks = lax.axis_size("ctx")
    quads = blocks // QUAD
    rows, channels = query_gate.shape
    lags = filter_taps.shape[1]
    piece = channels // (QUAD * quads * CHUNKS)
    width = quads * piece
    pos = lax.axis_index("ctx").astype(jnp.int32).reshape(1)
    table = jnp.asarray(tables(rows))
    aligned = piece % 128 == 0

    def grouped(array):
        if aligned:
            return array
        parts = array.reshape(rows, quads, QUAD, CHUNKS, piece)
        return parts.transpose(0, 2, 3, 1, 4).reshape(rows, channels)

    def ungrouped(array):
        if aligned:
            return array
        parts = array.reshape(rows, QUAD, CHUNKS, quads, piece)
        return parts.transpose(0, 3, 1, 2, 4).reshape(rows, channels)

    if aligned:
        pieces = (quads, piece)
        offset = lambda chunk, i, pair, side: (((2 * i + pair) * 2 + side) * CHUNKS + chunk) * piece
    else:
        pieces = (1, width)
        offset = lambda chunk, i, pair, side: ((2 * pair + side) * CHUNKS + chunk) * width

    def to_member(value, k):
        return lax.ppermute(value, "ctx", [(i, i ^ k) for i in range(blocks)]) if k else value

    def gate(values, *after):
        return pl.pallas_call(
            gate_kernel,
            out_shape=[jax.ShapeDtypeStruct(value.shape, value.dtype) for value in values],
            in_specs=[ANY] * (len(values) + len(after)),
            out_specs=[ANY] * len(values),
            input_output_aliases={n: n for n in range(len(values))},
            compiler_params=PARAMS,
            name="gate",
        )(*values, *after)

    def to_quad(value, s):
        return to_member(value, QUAD * s)

    key_branch, value_branch = grouped(key_branch), grouped(value_branch)
    out_grad, query_gate = grouped(out_grad), grouped(query_gate)
    parts, step = [filter_taps], quads // 2
    while step:
        held = parts[0] if len(parts) == 1 else jnp.concatenate(parts, axis=0)
        parts, step = [held, to_quad(held, step)], step // 2

    alone, both = jax.ShapeDtypeStruct((rows, width), BF16), jax.ShapeDtypeStruct((rows, CHUNKS * width), BF16)
    def products(kernel, left, right, types, limit, name):
        return pl.pallas_call(
            partial(kernel, pieces, offset),
            out_shape=types,
            in_specs=[SMEM] + [HBM] * 2,
            out_specs=[VMEM] * len(types),
            scratch_shapes=[pltpu.VMEM((rows, channels), BF16)] * 2 + [pltpu.SemaphoreType.DMA((2, pieces[0]))],
            compiler_params=pltpu.CompilerParams(vmem_limit_bytes=limit * 1024 * 1024),
            name=name,
        )(pos, left, right)

    own, near, same, other = products(grad_kernel, out_grad, query_gate, [both] * 4, 60, "gated_grad")
    grads = [own, to_member(near, 1), to_member(same, 2), to_member(other, 3)]
    pair = jax.ShapeDtypeStruct((2 * rows, width), BF16)
    own, near, *far_inputs = products(input_kernel, key_branch, value_branch, [both] * 2 + [pair] * CHUNKS, 40, "conv_input")
    own_input, near_input = own, near
    far_inputs = [to_member(value, 2) for value in far_inputs]
    spectra = pl.pallas_call(
        partial(filter_kernel, quads),
        out_shape=jax.ShapeDtypeStruct((REACH * lags, CHUNKS * width), F32),
        in_specs=[SMEM, VMEM] + [VMEM] * len(parts),
        out_specs=VMEM,
        scratch_shapes=[pltpu.VMEM((CHUNKS * width, lags), BF16)],
        compiler_params=PARAMS,
        name="filter_spectra",
    )(pos, table, *parts)
    first_blocks = pl.pallas_call(
        partial(halo_kernel, CHUNKS),
        out_shape=[jax.ShapeDtypeStruct((REACH * rows, width), BF16)] * CHUNKS,
        in_specs=[SMEM] + [VMEM] * QUAD,
        out_specs=[VMEM] * CHUNKS,
        compiler_params=PARAMS,
        name="halo",
    )(pos, *grads)
    before = first_blocks[0]
    results, chunk_grads, chunk_terms = [], [], []
    whole = lambda *shape: pl.BlockSpec(shape, lambda _: (0,) * len(shape))
    nearest = []
    for chunk in range(CHUNKS):
        halo = lax.ppermute(first_blocks[chunk], "ctx", [(i, i - QUAD) for i in range(QUAD, blocks)])
        share = pl.BlockSpec((rows, width), lambda _, chunk=chunk: (0, chunk))
        forward = pl.pallas_call(
            pack_kernel,
            grid=(1,),
            out_shape=jax.ShapeDtypeStruct((2 * rows, width), BF16),
            in_specs=[share, whole(2 * rows, width), ANY],
            out_specs=whole(2 * rows, width),
            compiler_params=PARAMS,
            name=f"pack_{chunk}",
        )(near_input, far_inputs[chunk], before)
        forward = to_member(forward, 1)
        done = pl.pallas_call(
            partial(conv_kernel, chunk, quads, doc_blocks.shape[0]),
            grid=(1,),
            out_shape=[alone] * QUAD
            + [jax.ShapeDtypeStruct((width // 2, lags), kind) for kind in (F32, BF16)],
            in_specs=[SMEM, SMEM, whole(*table.shape), whole(REACH * rows, width)]
            + [pl.BlockSpec((REACH * lags, width), lambda _, chunk=chunk: (0, chunk))]
            + [share] * (QUAD + 1)
            + [whole(2 * rows, width)] * 2,
            out_specs=[whole(rows, width)] * QUAD + [whole(width // 2, lags)] * 2,
            scratch_shapes=[
                pltpu.VMEM(((QUAD + REACH) * rows, width), BF16),
                pltpu.VMEM((QUAD * rows, width), BF16),
                pltpu.VMEM((QUAD * rows, width), BF16),
                pltpu.VMEM((width, lags), F32),
            ],
            compiler_params=PARAMS,
            name=f"conv_{chunk}",
        )(pos, doc_blocks, table, halo, spectra, *grads, own_input, far_inputs[chunk], forward)
        own, *sent, kept, send = done
        before = kept
        if chunk:
            *sent, send = gate([*sent, send], *chunk_grads[-1][2:], chunk_terms[-1][1])
        chunk_grads.append([own, *[to_member(value, k + 1) for k, value in enumerate(sent)]])
        chunk_terms.append((kept, to_quad(send, 1)))
    filter_grads = []
    for chunk in range(CHUNKS):
        gradients, (kept, came) = chunk_grads[chunk], chunk_terms[chunk]
        step = 1
        while 2 * step < quads:
            step *= 2
            half = kept.shape[0] // 2
            kept, send = pl.pallas_call(
                fold_kernel,
                out_shape=[jax.ShapeDtypeStruct((half, lags), kind) for kind in (F32, BF16)],
                in_specs=[VMEM] * 2 + [ANY] * len(filter_grads[-1:]),
                out_specs=[VMEM] * 2,
                compiler_params=PARAMS,
                name=f"fold_{chunk}_{step}",
            )(kept, came, *filter_grads[-1:])
            came = to_quad(send, step)
        filter_grads += [kept, came]
        last = filter_grads if chunk == CHUNKS - 1 else []
        results = pl.pallas_call(
            partial(final_kernel, chunk, pieces, offset, 1.0 / math.sqrt(rows * blocks), len(last)),
            out_shape=[jax.ShapeDtypeStruct((rows, channels), BF16)] * 2
            + [jax.ShapeDtypeStruct((CHUNKS * piece, lags), F32)] * (len(last) > 0),
            in_specs=[SMEM] + [VMEM] * (2 + QUAD + len(last)) + [HBM] * len(results),
            out_specs=[HBM] * (3 if last else 2),
            scratch_shapes=[
                pltpu.VMEM((CHUNKS * piece, lags), F32),
                pltpu.SemaphoreType.DMA,
                pltpu.VMEM((rows, QUAD * width), BF16),
                pltpu.VMEM((rows, QUAD * width), BF16),
                pltpu.SemaphoreType.DMA((2, QUAD * pieces[0])),
            ],
            input_output_aliases={3 + QUAD + len(last) + n: n for n in range(len(results))},
            compiler_params=PARAMS,
            name=f"gate_products_{chunk}",
        )(pos, key_branch, value_branch, *gradients, *last, *results)
    key_grad, value_grad, filter_grad = results
    return (ungrouped(key_grad), ungrouped(value_grad), filter_grad)


def solution(mesh):
    in_specs = (
        P(("groups", "ctx"), None),
        P(("groups", "ctx"), None),
        P(("groups", "ctx"), None),
        P(("groups", "ctx"), None),
        P("ctx", None),
        P("groups"),
    )
    out_specs = (P(("groups", "ctx"), None), P(("groups", "ctx"), None), P(("groups", "ctx"), None))
    return jax.shard_map(shards, mesh=mesh, in_specs=in_specs, out_specs=out_specs, check_vma=False)
```

```python
import math
from functools import partial

import jax
import jax.numpy as jnp
import ml_dtypes
import numpy as np
from jax import lax
from jax.experimental import pallas as pl
from jax.experimental.pallas import tpu as pltpu
from jax.sharding import PartitionSpec as P

QUAD = 4
CHUNKS = 2
REACH = 2
TILE = 256
F32 = jnp.float32
BF16 = jnp.bfloat16
SMEM = pl.BlockSpec(memory_space=pltpu.SMEM)
VMEM = pl.BlockSpec(memory_space=pltpu.VMEM)
HBM = pl.BlockSpec(memory_space=pltpu.HBM)
ANY = pl.BlockSpec(memory_space=pl.ANY)
PARAMS = pltpu.CompilerParams(vmem_limit_bytes=40 * 1024 * 1024)


def halving_order(count):
    order = [0]
    while len(order) < count:
        order = [2 * n for n in order] + [2 * n + 1 for n in order]
    return order


def split_bf16(table):
    high = table.astype(ml_dtypes.bfloat16)
    low = (table - high.astype(np.float64)).astype(ml_dtypes.bfloat16)
    return high, low


def tables(rows):
    length = 2 * rows
    omega = 2.0 * math.pi * (np.arange(rows) + 0.5) / length
    angle = omega[:, None] * np.arange(length)[None, :]
    forward = np.concatenate([np.cos(angle), -np.sin(angle)], axis=0)
    high, low = split_bf16(forward)
    half = np.concatenate([high[:, :rows], low[:, :rows]], axis=1)
    back_high, back_low = split_bf16(forward[:, :rows].T / rows)
    back = np.concatenate([back_high, back_low], axis=0)
    return np.concatenate([high, low, half, back], axis=0)


def dot(left, right):
    return jnp.dot(left, right, preferred_element_type=F32)


def conj_product(left, right):
    (lr, li), (rr, ri) = left, right
    return lr * rr + li * ri, li * rr - lr * ri


def halves(spectrum):
    rows = spectrum.shape[0] // 2
    return spectrum[:rows], spectrum[rows:]


def add(left, right):
    return left[0] + right[0], left[1] + right[1]


def invert(back, real, imag):
    rows = real.shape[0]
    spectrum = jnp.concatenate([real, imag], axis=0)
    both = dot(back, spectrum.astype(BF16))
    return both[:rows] + both[rows:]


def cut_products(pieces, offset, sources, held, sems, outs):
    count, width = pieces
    section = held[0].shape[1] // count
    copies = []
    for i in range(count):
        lanes = pl.ds(i * section, section)
        for n, (source, target) in enumerate(zip(sources, held)):
            copies.append(pltpu.make_async_copy(source.at[:, lanes], target.at[:, lanes], sems.at[n, i]))
            copies[-1].start()
    for i in range(count):
        copies[2 * i].wait()
        copies[2 * i + 1].wait()
        for out, side, pair, chunks in outs:
            for n, chunk in enumerate(chunks):
                lanes = pl.ds(pl.multiple_of(offset(chunk, i, pair, side), 128), width)
                first = (n * count + i) * width
                out[:, first : first + width] = held[0][:, lanes] * held[1][:, lanes]


def grad_kernel(pieces, offset, pos_ref, left_hbm, right_hbm, own, near, same, other, left_ref, right_ref, sems):
    place = pos_ref[0] % QUAD
    core, chip = place % 2, place // 2
    every = range(CHUNKS)
    outs = [(same, core, 1 - chip, every), (other, 1 - core, 1 - chip, every)]
    outs += [(near, 1 - core, chip, every), (own, core, chip, every)]
    cut_products(pieces, offset, (left_hbm, right_hbm), (left_ref, right_ref), sems, outs)


def input_kernel(pieces, offset, pos_ref, left_hbm, right_hbm, own, near, *refs):
    far, (left_ref, right_ref, sems) = refs[:-3], refs[-3:]
    rows = own.shape[0]
    place = pos_ref[0] % QUAD
    core, chip = place % 2, place // 2
    outs = [(near, 1 - core, chip, range(CHUNKS)), (own, core, chip, range(CHUNKS))]
    for chunk, out in enumerate(far):
        outs += [(out.at[:rows, :], core, 1 - chip, [chunk]), (out.at[rows:, :], 1 - core, 1 - chip, [chunk])]
    cut_products(pieces, offset, (left_hbm, right_hbm), (left_ref, right_ref), sems, outs)


def pack_kernel(chunk, near_ref, came_ref, *refs):
    out = refs[-1]
    rows, width = near_ref.shape[0], out.shape[1]
    out[:rows, :] = near_ref[:, chunk * width : (chunk + 1) * width]
    out[rows:, :] = came_ref[rows:, :]


def filter_kernel(quads, pos_ref, table_ref, *refs):
    parts, out, taps_all = refs[:-2], refs[-2], refs[-1]
    quad = pos_ref[0] // QUAD
    channels, lags = taps_all.shape
    rows = lags // REACH
    half = table_ref[2 * lags : 3 * lags]
    width = channels // CHUNKS
    piece = width // quads
    held = [(part, at) for part in parts for at in range(0, part.shape[0], CHUNKS * piece)]
    for s, (part, first) in zip(halving_order(quads), held):
        for chunk in range(CHUNKS):
            at = pl.ds(pl.multiple_of(chunk * width + lax.bitwise_xor(quad, s) * piece, piece), piece)
            taps_all[at, :] = part[first + chunk * piece : first + (chunk + 1) * piece, :]
    for first in range(0, channels, TILE):
        for segment in range(REACH):
            taps = taps_all[first : first + TILE, segment * rows : (segment + 1) * rows]
            twice = jnp.concatenate([taps, taps], axis=1)
            spectrum = lax.dot_general(half, twice, (((1,), (1,)), ((), ())), preferred_element_type=F32)
            out[segment * lags : (segment + 1) * lags, first : first + TILE] = spectrum


def gate_kernel(*refs):
    del refs


def halo_kernel(chunks, pos_ref, *refs):
    place = pos_ref[0] % QUAD
    held, outs = refs[:QUAD], refs[-chunks:]
    rows, width = held[0].shape[0], outs[0].shape[1]
    for block in range(REACH):
        for k in range(QUAD):

            @pl.when(lax.bitwise_xor(place, k) == block)
            def _():
                for chunk, out in enumerate(outs):
                    out[block * rows : (block + 1) * rows, :] = held[k][:rows, chunk * width : (chunk + 1) * width]


def joined_blocks(pos_ref, docs_ref, docs):
    joined = []
    for j in range(QUAD + 1):
        same, end = jnp.int32(1), jnp.int32(0)
        for d in range(docs):
            end = end + docs_ref[d]
            same = jnp.where(end == pos_ref[0] // QUAD * QUAD + j + 1, 0, same)
        joined.append(same.astype(F32))
    return joined


def convolve(joined, table_ref, filters, grad_of, input_of, put):
    length = table_ref.shape[1]
    half, back = table_ref[2 * length : 3 * length], table_ref[3 * length :]
    windows = []
    for j in range(QUAD + 1):
        both = jnp.concatenate([grad_of(j), grad_of(j + 1) * joined[j].astype(BF16)], axis=0)
        parts = dot(table_ref[: 2 * length], both)
        windows.append(parts[:length] + parts[length:])
    sums = None
    for j in range(QUAD):
        near, far = halves(windows[j]), halves(windows[j + 1] * joined[j])
        real, imag = add(conj_product(near, filters[0]), conj_product(far, filters[1]))
        put(j, invert(back, real, imag).astype(BF16))
        held = input_of(j)
        source = halves(dot(half, jnp.concatenate([held, held], axis=0)))
        terms = [conj_product(near, source), conj_product(far, source)]
        sums = [add(*pair) for pair in zip(sums, terms)] if sums else terms
    return sums


def tiles(width):
    return [slice(first, min(first + TILE, width)) for first in range(0, width, TILE)]


def conv_kernel(chunk, quads, docs, pos_ref, docs_ref, table_ref, filter_ref, halo_ref, *refs):
    grads, (own_ref, far_ref, came_ref) = refs[:QUAD], refs[QUAD : QUAD + 3]
    outs, terms = refs[-6 - QUAD : -6], refs[-6:-4]
    grad_all, input_all, out_all, terms_all = refs[-4:]
    rows, width = outs[0].shape
    length = 2 * rows
    piece = width // quads
    place, quad = pos_ref[0] % QUAD, pos_ref[0] // QUAD
    share = slice(chunk * width, (chunk + 1) * width)
    joined = joined_blocks(pos_ref, docs_ref, docs)
    for k in range(QUAD):
        at = pl.ds(pl.multiple_of(lax.bitwise_xor(place, k) * rows, rows), rows)
        grad_all[at, :] = grads[k][:, share]
        if k:
            held = (far_ref if k == 2 else came_ref)[k // 3 * rows : (k // 3 + 1) * rows, :]
        else:
            held = own_ref[:, share]
        input_all[at, :] = held
    grad_all[QUAD * rows :, :] = halo_ref[...]
    for lanes in tiles(width):

        def put(j, value, lanes=lanes):
            out_all[j * rows : (j + 1) * rows, lanes] = value

        of_chunk = slice(chunk * width + lanes.start, chunk * width + lanes.stop)
        filters = [halves(filter_ref[n * length : (n + 1) * length, of_chunk]) for n in range(REACH)]
        block = lambda ref, j, lanes=lanes: ref[j * rows : (j + 1) * rows, lanes]
        sums = convolve(joined, table_ref, filters, partial(block, grad_all), partial(block, input_all), put)
        for segment in range(REACH):
            lags = invert(table_ref[3 * length :], *sums[segment])
            terms_all[lanes, segment * rows : (segment + 1) * rows] = lags.T
    for k in range(QUAD):
        at = pl.ds(pl.multiple_of(lax.bitwise_xor(place, k) * rows, rows), rows)
        if k == 1 and chunk:
            outs[k][:, : chunk * width] = refs[QUAD + 3][...]
            outs[k][:, chunk * width :] = out_all[at, :]
        else:
            outs[k][...] = out_all[at, :]
    for n, s in enumerate(halving_order(quads)):
        at = pl.ds(pl.multiple_of(lax.bitwise_xor(quad, s) * piece, piece), piece)
        sent, n = divmod(n, quads // 2)
        terms[sent][n * piece : (n + 1) * piece, :] = terms_all[at, :].astype(terms[sent].dtype)


def fold_kernel(kept_ref, came_ref, keep_ref, send_ref):
    half = keep_ref.shape[0]
    keep_ref[...] = kept_ref[:half, :] + came_ref[:half, :].astype(F32)
    send_ref[...] = (kept_ref[half:, :] + came_ref[half:, :].astype(F32)).astype(BF16)


def final_kernel(chunk, pieces, offset, scale, terms, pos_ref, key_ref, value_ref, *refs):
    grads, filters = refs[:QUAD], refs[QUAD : QUAD + terms]
    filter_all, filter_sem, key_all, value_all, sems = refs[-5:]
    key_out, value_out, *filter_out = refs[-8 if terms else -7 : -5]
    place = pos_ref[0] % QUAD
    count, width = pieces
    copies = []
    for n in range(terms // 2):
        kept, came = filters[2 * n], filters[2 * n + 1]
        rows = kept.shape[0]
        filter_all[n * rows : (n + 1) * rows, :] = (kept[...] + came[...].astype(F32)) * scale
    for out in filter_out:
        copies.append(pltpu.make_async_copy(filter_all, out, filter_sem))
        copies[-1].start()
    for k in range(QUAD):
        member = lax.bitwise_xor(place, k)
        for i in range(count):
            n = k * count + i
            lanes = pl.ds(pl.multiple_of(offset(chunk, i, member // 2, member % 2), 128), width)
            held = slice(n * width, (n + 1) * width)
            first = ((chunk * count if k == 1 else 0) + i) * width
            grad = grads[k][:, first : first + width]
            key_all[:, held] = grad * value_ref[:, lanes]
            value_all[:, held] = grad * key_ref[:, lanes]
            copies.append(pltpu.make_async_copy(key_all.at[:, held], key_out.at[:, lanes], sems.at[0, n]))
            copies.append(pltpu.make_async_copy(value_all.at[:, held], value_out.at[:, lanes], sems.at[1, n]))
            copies[-2].start()
            copies[-1].start()
    for copy in copies:
        copy.wait()


def shards(query_gate, key_branch, value_branch, out_grad, filter_taps, doc_blocks):
    blocks = lax.axis_size("ctx")
    quads = blocks // QUAD
    rows, channels = query_gate.shape
    lags = filter_taps.shape[1]
    piece = channels // (QUAD * quads * CHUNKS)
    width = quads * piece
    pos = lax.axis_index("ctx").astype(jnp.int32).reshape(1)
    table = jnp.asarray(tables(rows))
    aligned = piece % 128 == 0

    def grouped(array):
        if aligned:
            return array
        parts = array.reshape(rows, quads, QUAD, CHUNKS, piece)
        return parts.transpose(0, 2, 3, 1, 4).reshape(rows, channels)

    def ungrouped(array):
        if aligned:
            return array
        parts = array.reshape(rows, QUAD, CHUNKS, quads, piece)
        return parts.transpose(0, 3, 1, 2, 4).reshape(rows, channels)

    if aligned:
        pieces = (quads, piece)
        offset = lambda chunk, i, pair, side: (((2 * i + pair) * 2 + side) * CHUNKS + chunk) * piece
    else:
        pieces = (1, width)
        offset = lambda chunk, i, pair, side: ((2 * pair + side) * CHUNKS + chunk) * width

    def to_member(value, k):
        return lax.ppermute(value, "ctx", [(i, i ^ k) for i in range(blocks)]) if k else value

    def gate(values, *after):
        return pl.pallas_call(
            gate_kernel,
            out_shape=[jax.ShapeDtypeStruct(value.shape, value.dtype) for value in values],
            in_specs=[ANY] * (len(values) + len(after)),
            out_specs=[ANY] * len(values),
            input_output_aliases={n: n for n in range(len(values))},
            compiler_params=PARAMS,
            name="gate",
        )(*values, *after)

    def to_quad(value, s):
        return to_member(value, QUAD * s)

    key_branch, value_branch = grouped(key_branch), grouped(value_branch)
    out_grad, query_gate = grouped(out_grad), grouped(query_gate)
    parts, step = [filter_taps], quads // 2
    while step:
        held = parts[0] if len(parts) == 1 else jnp.concatenate(parts, axis=0)
        parts, step = [held, to_quad(held, step)], step // 2

    alone, both = jax.ShapeDtypeStruct((rows, width), BF16), jax.ShapeDtypeStruct((rows, CHUNKS * width), BF16)
    def products(kernel, left, right, types, limit, name):
        return pl.pallas_call(
            partial(kernel, pieces, offset),
            out_shape=types,
            in_specs=[SMEM] + [HBM] * 2,
            out_specs=[VMEM] * len(types),
            scratch_shapes=[pltpu.VMEM((rows, channels), BF16)] * 2 + [pltpu.SemaphoreType.DMA((2, pieces[0]))],
            compiler_params=pltpu.CompilerParams(vmem_limit_bytes=limit * 1024 * 1024),
            name=name,
        )(pos, left, right)

    own, near, same, other = products(grad_kernel, out_grad, query_gate, [both] * 4, 60, "gated_grad")
    grads = [own, to_member(near, 1), to_member(same, 2), to_member(other, 3)]
    pair_type = jax.ShapeDtypeStruct((2 * rows, width), BF16)
    own, near, *far_inputs = products(input_kernel, key_branch, value_branch, [both] * 2 + [pair_type] * CHUNKS, 40, "conv_input")
    own_input, near_input = own, near
    far_inputs = [to_member(value, 2) for value in far_inputs]
    spectra = pl.pallas_call(
        partial(filter_kernel, quads),
        out_shape=jax.ShapeDtypeStruct((REACH * lags, CHUNKS * width), F32),
        in_specs=[SMEM, VMEM] + [VMEM] * len(parts),
        out_specs=VMEM,
        scratch_shapes=[pltpu.VMEM((CHUNKS * width, lags), BF16)],
        compiler_params=PARAMS,
        name="filter_spectra",
    )(pos, table, *parts)
    first_blocks = pl.pallas_call(
        partial(halo_kernel, CHUNKS),
        out_shape=[jax.ShapeDtypeStruct((REACH * rows, width), BF16)] * CHUNKS,
        in_specs=[SMEM] + [VMEM] * QUAD,
        out_specs=[VMEM] * CHUNKS,
        compiler_params=PARAMS,
        name="halo",
    )(pos, *grads)
    before = [first_blocks[0]]
    results, chunk_grads, chunk_terms = [], [], []
    nearest = []
    for chunk in range(CHUNKS):
        halo = lax.ppermute(first_blocks[chunk], "ctx", [(i, i - QUAD) for i in range(QUAD, blocks)])
        forward = pl.pallas_call(
            partial(pack_kernel, chunk),
            out_shape=pair_type,
            in_specs=[VMEM, VMEM] + [ANY] * len(before),
            out_specs=VMEM,
            compiler_params=PARAMS,
            name=f"pack_{chunk}",
        )(near_input, far_inputs[chunk], *before)
        forward = to_member(forward, 1)
        done = pl.pallas_call(
            partial(conv_kernel, chunk, quads, doc_blocks.shape[0]),
            out_shape=[alone, jax.ShapeDtypeStruct((rows, (chunk + 1) * width), BF16), alone, alone]
            + [jax.ShapeDtypeStruct((width // 2, lags), kind) for kind in (F32, BF16)],
            in_specs=[SMEM, SMEM] + [VMEM] * (6 + QUAD + len(nearest)),
            out_specs=[VMEM] * (QUAD + 2),
            scratch_shapes=[
                pltpu.VMEM(((QUAD + REACH) * rows, width), BF16),
                pltpu.VMEM((QUAD * rows, width), BF16),
                pltpu.VMEM((QUAD * rows, width), BF16),
                pltpu.VMEM((width, lags), F32),
            ],
            compiler_params=PARAMS,
            name=f"conv_{chunk}",
        )(pos, doc_blocks, table, spectra, halo, *grads, own_input, far_inputs[chunk], forward, *nearest)
        own, pair, *sent, kept, send = done
        before, nearest = [kept], [pair]
        if chunk:
            *sent, pair, send = gate([*sent, pair, send], *chunk_grads[-1][2:], chunk_terms[-1][1])
        chunk_grads.append([own, pair, *[to_member(value, 2 + k) for k, value in enumerate(sent)]])
        chunk_terms.append((kept, to_quad(send, 1)))
    nearest = to_member(pair, 1)
    filter_grads = []
    for chunk in range(CHUNKS):
        gradients, (kept, came) = chunk_grads[chunk], chunk_terms[chunk]
        gradients[1] = nearest
        step = 1
        while 2 * step < quads:
            step *= 2
            half = kept.shape[0] // 2
            kept, send = pl.pallas_call(
                fold_kernel,
                out_shape=[jax.ShapeDtypeStruct((half, lags), kind) for kind in (F32, BF16)],
                in_specs=[VMEM] * 2,
                out_specs=[VMEM] * 2,
                compiler_params=PARAMS,
                name=f"fold_{chunk}_{step}",
            )(kept, came)
            came = to_quad(send, step)
        filter_grads += [kept, came]
        last = filter_grads if chunk == CHUNKS - 1 else []
        results = pl.pallas_call(
            partial(final_kernel, chunk, pieces, offset, 1.0 / math.sqrt(rows * blocks), len(last)),
            out_shape=[jax.ShapeDtypeStruct((rows, channels), BF16)] * 2
            + [jax.ShapeDtypeStruct((CHUNKS * piece, lags), F32)] * (len(last) > 0),
            in_specs=[SMEM] + [VMEM] * (2 + QUAD + len(last)) + [HBM] * len(results),
            out_specs=[HBM] * (3 if last else 2),
            scratch_shapes=[
                pltpu.VMEM((CHUNKS * piece, lags), F32),
                pltpu.SemaphoreType.DMA,
                pltpu.VMEM((rows, QUAD * width), BF16),
                pltpu.VMEM((rows, QUAD * width), BF16),
                pltpu.SemaphoreType.DMA((2, QUAD * pieces[0])),
            ],
            input_output_aliases={3 + QUAD + len(last) + n: n for n in range(len(results))},
            compiler_params=PARAMS,
            name=f"gate_products_{chunk}",
        )(pos, key_branch, value_branch, *gradients, *last, *results)
    key_grad, value_grad, filter_grad = results
    return (ungrouped(key_grad), ungrouped(value_grad), filter_grad)


def solution(mesh):
    in_specs = (
        P(("groups", "ctx"), None),
        P(("groups", "ctx"), None),
        P(("groups", "ctx"), None),
        P(("groups", "ctx"), None),
        P("ctx", None),
        P("groups"),
    )
    out_specs = (P(("groups", "ctx"), None), P(("groups", "ctx"), None), P(("groups", "ctx"), None))
    return jax.shard_map(shards, mesh=mesh, in_specs=in_specs, out_specs=out_specs, check_vma=False)
```

```python
import math
from functools import partial

import jax
import jax.numpy as jnp
import ml_dtypes
import numpy as np
from jax import lax
from jax.experimental import pallas as pl
from jax.experimental.pallas import tpu as pltpu
from jax.sharding import PartitionSpec as P

QUAD = 4
CHUNKS = 2
REACH = 2
TILE = 256
F32 = jnp.float32
BF16 = jnp.bfloat16
SMEM = pl.BlockSpec(memory_space=pltpu.SMEM)
VMEM = pl.BlockSpec(memory_space=pltpu.VMEM)
HBM = pl.BlockSpec(memory_space=pltpu.HBM)
ANY = pl.BlockSpec(memory_space=pl.ANY)
PARAMS = pltpu.CompilerParams(vmem_limit_bytes=40 * 1024 * 1024)


def halving_order(count):
    order = [0]
    while len(order) < count:
        order = [2 * n for n in order] + [2 * n + 1 for n in order]
    return order


def split_bf16(table):
    high = table.astype(ml_dtypes.bfloat16)
    low = (table - high.astype(np.float64)).astype(ml_dtypes.bfloat16)
    return high, low


def tables(rows):
    length = 2 * rows
    omega = 2.0 * math.pi * (np.arange(rows) + 0.5) / length
    angle = omega[:, None] * np.arange(length)[None, :]
    forward = np.concatenate([np.cos(angle), -np.sin(angle)], axis=0)
    high, low = split_bf16(forward)
    half = np.concatenate([high[:, :rows], low[:, :rows]], axis=1)
    back_high, back_low = split_bf16(forward[:, :rows].T / rows)
    back = np.concatenate([back_high, back_low], axis=0)
    return np.concatenate([high, low, half, back], axis=0)


def dot(left, right):
    return jnp.dot(left, right, preferred_element_type=F32)


def conj_product(left, right):
    (lr, li), (rr, ri) = left, right
    return lr * rr + li * ri, li * rr - lr * ri


def halves(spectrum):
    rows = spectrum.shape[0] // 2
    return spectrum[:rows], spectrum[rows:]


def add(left, right):
    return left[0] + right[0], left[1] + right[1]


def invert(back, real, imag):
    rows = real.shape[0]
    spectrum = jnp.concatenate([real, imag], axis=0)
    both = dot(back, spectrum.astype(BF16))
    return both[:rows] + both[rows:]


def cut_products(pieces, offset, sources, held, sems, outs):
    count, width = pieces
    section = held[0].shape[1] // count
    copies = []
    for i in range(count):
        lanes = pl.ds(i * section, section)
        for n, (source, target) in enumerate(zip(sources, held)):
            copies.append(pltpu.make_async_copy(source.at[:, lanes], target.at[:, lanes], sems.at[n, i]))
            copies[-1].start()
    for i in range(count):
        copies[2 * i].wait()
        copies[2 * i + 1].wait()
        for out, side, pair, chunks in outs:
            for n, chunk in enumerate(chunks):
                lanes = pl.ds(pl.multiple_of(offset(chunk, i, pair, side), 128), width)
                first = (n * count + i) * width
                out[:, first : first + width] = held[0][:, lanes] * held[1][:, lanes]


def grad_kernel(pieces, offset, pos_ref, left_hbm, right_hbm, own, near, same, other, left_ref, right_ref, sems):
    place = pos_ref[0] % QUAD
    core, chip = place % 2, place // 2
    every = range(CHUNKS)
    outs = [(same, core, 1 - chip, every), (other, 1 - core, 1 - chip, every)]
    outs += [(near, 1 - core, chip, every), (own, core, chip, every)]
    cut_products(pieces, offset, (left_hbm, right_hbm), (left_ref, right_ref), sems, outs)


def input_kernel(pieces, offset, pos_ref, left_hbm, right_hbm, _, own, near, *refs):
    far, (left_ref, right_ref, sems) = refs[:-3], refs[-3:]
    rows = own.shape[0]
    place = pos_ref[0] % QUAD
    core, chip = place % 2, place // 2
    outs = [(near, 1 - core, chip, range(CHUNKS)), (own, core, chip, range(CHUNKS))]
    for chunk, out in enumerate(far):
        outs += [(out.at[:rows, :], core, 1 - chip, [chunk]), (out.at[rows:, :], 1 - core, 1 - chip, [chunk])]
    cut_products(pieces, offset, (left_hbm, right_hbm), (left_ref, right_ref), sems, outs)


def pack_kernel(chunk, near_ref, came_ref, *refs):
    out = refs[-1]
    rows, width = near_ref.shape[0], out.shape[1]
    out[:rows, :] = near_ref[:, chunk * width : (chunk + 1) * width]
    out[rows:, :] = came_ref[rows:, :]


def filter_kernel(quads, pos_ref, table_ref, *refs):
    parts, out, taps_all = refs[:-2], refs[-2], refs[-1]
    quad = pos_ref[0] // QUAD
    channels, lags = taps_all.shape
    rows = lags // REACH
    half = table_ref[2 * lags : 3 * lags]
    width = channels // CHUNKS
    piece = width // quads
    held = [(part, at) for part in parts for at in range(0, part.shape[0], CHUNKS * piece)]
    for s, (part, first) in zip(halving_order(quads), held):
        for chunk in range(CHUNKS):
            at = pl.ds(pl.multiple_of(chunk * width + lax.bitwise_xor(quad, s) * piece, piece), piece)
            taps_all[at, :] = part[first + chunk * piece : first + (chunk + 1) * piece, :]
    for first in range(0, channels, TILE):
        for segment in range(REACH):
            taps = taps_all[first : first + TILE, segment * rows : (segment + 1) * rows]
            twice = jnp.concatenate([taps, taps], axis=1)
            spectrum = lax.dot_general(half, twice, (((1,), (1,)), ((), ())), preferred_element_type=F32)
            out[segment * lags : (segment + 1) * lags, first : first + TILE] = spectrum


def gate_kernel(*refs):
    del refs


def halo_kernel(chunks, pos_ref, *refs):
    place = pos_ref[0] % QUAD
    held, outs = refs[:QUAD], refs[-chunks:]
    rows, width = held[0].shape[0], outs[0].shape[1]
    for block in range(REACH):
        for k in range(QUAD):

            @pl.when(lax.bitwise_xor(place, k) == block)
            def _():
                for chunk, out in enumerate(outs):
                    out[block * rows : (block + 1) * rows, :] = held[k][:rows, chunk * width : (chunk + 1) * width]


def joined_blocks(pos_ref, docs_ref, docs):
    joined = []
    for j in range(QUAD + 1):
        same, end = jnp.int32(1), jnp.int32(0)
        for d in range(docs):
            end = end + docs_ref[d]
            same = jnp.where(end == pos_ref[0] // QUAD * QUAD + j + 1, 0, same)
        joined.append(same.astype(F32))
    return joined


def convolve(joined, table_ref, filters, grad_of, input_of, put):
    length = table_ref.shape[1]
    half, back = table_ref[2 * length : 3 * length], table_ref[3 * length :]
    windows = []
    for j in range(QUAD + 1):
        both = jnp.concatenate([grad_of(j), grad_of(j + 1) * joined[j].astype(BF16)], axis=0)
        parts = dot(table_ref[: 2 * length], both)
        windows.append(parts[:length] + parts[length:])
    sums = None
    for j in range(QUAD):
        near, far = halves(windows[j]), halves(windows[j + 1] * joined[j])
        real, imag = add(conj_product(near, filters[0]), conj_product(far, filters[1]))
        put(j, invert(back, real, imag).astype(BF16))
        held = input_of(j)
        source = halves(dot(half, jnp.concatenate([held, held], axis=0)))
        terms = [conj_product(near, source), conj_product(far, source)]
        sums = [add(*pair) for pair in zip(sums, terms)] if sums else terms
    return sums


def tiles(width):
    return [slice(first, min(first + TILE, width)) for first in range(0, width, TILE)]


def conv_kernel(chunk, quads, docs, pos_ref, docs_ref, table_ref, filter_ref, halo_ref, *refs):
    grads, (own_ref, far_ref, came_ref) = refs[:QUAD], refs[QUAD : QUAD + 3]
    outs, terms = refs[-6 - QUAD : -6], refs[-6:-4]
    grad_all, input_all, out_all, terms_all = refs[-4:]
    rows, width = outs[0].shape
    length = 2 * rows
    piece = width // quads
    place, quad = pos_ref[0] % QUAD, pos_ref[0] // QUAD
    share = slice(chunk * width, (chunk + 1) * width)
    joined = joined_blocks(pos_ref, docs_ref, docs)
    for k in range(QUAD):
        at = pl.ds(pl.multiple_of(lax.bitwise_xor(place, k) * rows, rows), rows)
        grad_all[at, :] = grads[k][:, share]
        if k:
            held = (far_ref if k == 2 else came_ref)[k // 3 * rows : (k // 3 + 1) * rows, :]
        else:
            held = own_ref[:, share]
        input_all[at, :] = held
    grad_all[QUAD * rows :, :] = halo_ref[...]
    for lanes in tiles(width):

        def put(j, value, lanes=lanes):
            out_all[j * rows : (j + 1) * rows, lanes] = value

        of_chunk = slice(chunk * width + lanes.start, chunk * width + lanes.stop)
        filters = [halves(filter_ref[n * length : (n + 1) * length, of_chunk]) for n in range(REACH)]
        block = lambda ref, j, lanes=lanes: ref[j * rows : (j + 1) * rows, lanes]
        sums = convolve(joined, table_ref, filters, partial(block, grad_all), partial(block, input_all), put)
        for segment in range(REACH):
            lags = invert(table_ref[3 * length :], *sums[segment])
            terms_all[lanes, segment * rows : (segment + 1) * rows] = lags.T
    for k in range(QUAD):
        at = pl.ds(pl.multiple_of(lax.bitwise_xor(place, k) * rows, rows), rows)
        if k == 1 and chunk:
            outs[k][:, : chunk * width] = refs[QUAD + 3][...]
            outs[k][:, chunk * width :] = out_all[at, :]
        else:
            outs[k][...] = out_all[at, :]
    for n, s in enumerate(halving_order(quads)):
        at = pl.ds(pl.multiple_of(lax.bitwise_xor(quad, s) * piece, piece), piece)
        sent, n = divmod(n, quads // 2)
        terms[sent][n * piece : (n + 1) * piece, :] = terms_all[at, :].astype(terms[sent].dtype)


def fold_kernel(kept_ref, came_ref, keep_ref, send_ref):
    half = keep_ref.shape[0]
    keep_ref[...] = kept_ref[:half, :] + came_ref[:half, :].astype(F32)
    send_ref[...] = (kept_ref[half:, :] + came_ref[half:, :].astype(F32)).astype(BF16)


def final_kernel(chunk, pieces, offset, scale, terms, pos_ref, key_ref, value_ref, *refs):
    grads, filters = refs[:QUAD], refs[QUAD : QUAD + terms]
    filter_all, filter_sem, key_all, value_all, sems = refs[-5:]
    key_out, value_out, *filter_out = refs[-8 if terms else -7 : -5]
    place = pos_ref[0] % QUAD
    count, width = pieces
    copies = []
    for n in range(terms // 2):
        kept, came = filters[2 * n], filters[2 * n + 1]
        rows = kept.shape[0]
        filter_all[n * rows : (n + 1) * rows, :] = (kept[...] + came[...].astype(F32)) * scale
    for out in filter_out:
        copies.append(pltpu.make_async_copy(filter_all, out, filter_sem))
        copies[-1].start()
    for k in range(QUAD):
        member = lax.bitwise_xor(place, k)
        for i in range(count):
            n = k * count + i
            lanes = pl.ds(pl.multiple_of(offset(chunk, i, member // 2, member % 2), 128), width)
            held = slice(n * width, (n + 1) * width)
            first = ((chunk * count if k == 1 else 0) + i) * width
            grad = grads[k][:, first : first + width]
            key_all[:, held] = grad * value_ref[:, lanes]
            value_all[:, held] = grad * key_ref[:, lanes]
            copies.append(pltpu.make_async_copy(key_all.at[:, held], key_out.at[:, lanes], sems.at[0, n]))
            copies.append(pltpu.make_async_copy(value_all.at[:, held], value_out.at[:, lanes], sems.at[1, n]))
            copies[-2].start()
            copies[-1].start()
    for copy in copies:
        copy.wait()


def shards(query_gate, key_branch, value_branch, out_grad, filter_taps, doc_blocks):
    blocks = lax.axis_size("ctx")
    quads = blocks // QUAD
    rows, channels = query_gate.shape
    lags = filter_taps.shape[1]
    piece = channels // (QUAD * quads * CHUNKS)
    width = quads * piece
    pos = lax.axis_index("ctx").astype(jnp.int32).reshape(1)
    table = jnp.asarray(tables(rows))
    aligned = piece % 128 == 0

    def grouped(array):
        if aligned:
            return array
        parts = array.reshape(rows, quads, QUAD, CHUNKS, piece)
        return parts.transpose(0, 2, 3, 1, 4).reshape(rows, channels)

    def ungrouped(array):
        if aligned:
            return array
        parts = array.reshape(rows, QUAD, CHUNKS, quads, piece)
        return parts.transpose(0, 3, 1, 2, 4).reshape(rows, channels)

    if aligned:
        pieces = (quads, piece)
        offset = lambda chunk, i, pair, side: (((2 * i + pair) * 2 + side) * CHUNKS + chunk) * piece
    else:
        pieces = (1, width)
        offset = lambda chunk, i, pair, side: ((2 * pair + side) * CHUNKS + chunk) * width

    def to_member(value, k):
        return lax.ppermute(value, "ctx", [(i, i ^ k) for i in range(blocks)]) if k else value

    def gate(values, *after):
        return pl.pallas_call(
            gate_kernel,
            out_shape=[jax.ShapeDtypeStruct(value.shape, value.dtype) for value in values],
            in_specs=[ANY] * (len(values) + len(after)),
            out_specs=[ANY] * len(values),
            input_output_aliases={n: n for n in range(len(values))},
            compiler_params=PARAMS,
            name="gate",
        )(*values, *after)

    def to_quad(value, s):
        return to_member(value, QUAD * s)

    key_branch, value_branch = grouped(key_branch), grouped(value_branch)
    out_grad, query_gate = grouped(out_grad), grouped(query_gate)
    parts, step = [filter_taps], quads // 2
    while step > 1:
        held = parts[0] if len(parts) == 1 else jnp.concatenate(parts, axis=0)
        parts, step = [held, to_quad(held, step)], step // 2
    if quads > 1:
        first = to_quad(parts[0], 1)
        parts += [first, *[to_quad(gate([part], first)[0], 1) for part in parts[1:]]]

    alone, both = jax.ShapeDtypeStruct((rows, width), BF16), jax.ShapeDtypeStruct((rows, CHUNKS * width), BF16)
    def products(kernel, left, right, types, limit, name, *after):
        return pl.pallas_call(
            partial(kernel, pieces, offset),
            out_shape=types,
            in_specs=[SMEM] + [HBM] * 2 + [ANY] * len(after),
            out_specs=[VMEM] * len(types),
            scratch_shapes=[pltpu.VMEM((rows, channels), BF16)] * 2 + [pltpu.SemaphoreType.DMA((2, pieces[0]))],
            compiler_params=pltpu.CompilerParams(vmem_limit_bytes=limit * 1024 * 1024),
            name=name,
        )(pos, left, right, *after)

    own, near, same, other = products(grad_kernel, out_grad, query_gate, [both] * 4, 60, "gated_grad")
    grads = [own, to_member(near, 1), to_member(same, 2), to_member(other, 3)]
    pair_type = jax.ShapeDtypeStruct((2 * rows, width), BF16)
    own, near, *far_inputs = products(input_kernel, key_branch, value_branch, [both] * 2 + [pair_type] * CHUNKS, 40, "conv_input", grads[1])
    own_input, near_input = own, near
    far_inputs = [to_member(value, 2) for value in far_inputs]
    spectra = pl.pallas_call(
        partial(filter_kernel, quads),
        out_shape=jax.ShapeDtypeStruct((REACH * lags, CHUNKS * width), F32),
        in_specs=[SMEM, VMEM] + [VMEM] * len(parts),
        out_specs=VMEM,
        scratch_shapes=[pltpu.VMEM((CHUNKS * width, lags), BF16)],
        compiler_params=PARAMS,
        name="filter_spectra",
    )(pos, table, *parts)
    first_blocks = pl.pallas_call(
        partial(halo_kernel, CHUNKS),
        out_shape=[jax.ShapeDtypeStruct((REACH * rows, width), BF16)] * CHUNKS,
        in_specs=[SMEM] + [VMEM] * QUAD,
        out_specs=[VMEM] * CHUNKS,
        compiler_params=PARAMS,
        name="halo",
    )(pos, *grads)
    before = [first_blocks[0], spectra]
    results, chunk_grads, chunk_terms = [], [], []
    nearest = []
    for chunk in range(CHUNKS):
        halo = lax.ppermute(first_blocks[chunk], "ctx", [(i, i - QUAD) for i in range(QUAD, blocks)])
        forward = pl.pallas_call(
            partial(pack_kernel, chunk),
            out_shape=pair_type,
            in_specs=[VMEM, VMEM] + [ANY] * len(before),
            out_specs=VMEM,
            compiler_params=PARAMS,
            name=f"pack_{chunk}",
        )(near_input, far_inputs[chunk], *before)
        forward = to_member(forward, 1)
        done = pl.pallas_call(
            partial(conv_kernel, chunk, quads, doc_blocks.shape[0]),
            out_shape=[alone, jax.ShapeDtypeStruct((rows, (chunk + 1) * width), BF16), alone, alone]
            + [jax.ShapeDtypeStruct((width // 2, lags), kind) for kind in (F32, BF16)],
            in_specs=[SMEM, SMEM] + [VMEM] * (6 + QUAD + len(nearest)),
            out_specs=[VMEM] * (QUAD + 2),
            scratch_shapes=[
                pltpu.VMEM(((QUAD + REACH) * rows, width), BF16),
                pltpu.VMEM((QUAD * rows, width), BF16),
                pltpu.VMEM((QUAD * rows, width), BF16),
                pltpu.VMEM((width, lags), F32),
            ],
            compiler_params=PARAMS,
            name=f"conv_{chunk}",
        )(pos, doc_blocks, table, spectra, halo, *grads, own_input, far_inputs[chunk], forward, *nearest)
        own, pair, *sent, kept, send = done
        before, nearest = [kept], [pair]
        if chunk:
            *sent, pair, send = gate([*sent, pair, send], *chunk_grads[-1][2:], chunk_terms[-1][1])
        chunk_grads.append([own, pair, *[to_member(value, 2 + k) for k, value in enumerate(sent)]])
        chunk_terms.append((kept, to_quad(send, 1)))
    nearest = to_member(pair, 1)
    filter_grads = []
    for chunk in range(CHUNKS):
        gradients, (kept, came) = chunk_grads[chunk], chunk_terms[chunk]
        gradients[1] = nearest
        step = 1
        while 2 * step < quads:
            step *= 2
            half = kept.shape[0] // 2
            kept, send = pl.pallas_call(
                fold_kernel,
                out_shape=[jax.ShapeDtypeStruct((half, lags), kind) for kind in (F32, BF16)],
                in_specs=[VMEM] * 2,
                out_specs=[VMEM] * 2,
                compiler_params=PARAMS,
                name=f"fold_{chunk}_{step}",
            )(kept, came)
            came = to_quad(send, step)
        filter_grads += [kept, came]
        last = filter_grads if chunk == CHUNKS - 1 else []
        results = pl.pallas_call(
            partial(final_kernel, chunk, pieces, offset, 1.0 / math.sqrt(rows * blocks), len(last)),
            out_shape=[jax.ShapeDtypeStruct((rows, channels), BF16)] * 2
            + [jax.ShapeDtypeStruct((CHUNKS * piece, lags), F32)] * (len(last) > 0),
            in_specs=[SMEM] + [VMEM] * (2 + QUAD + len(last)) + [HBM] * len(results),
            out_specs=[HBM] * (3 if last else 2),
            scratch_shapes=[
                pltpu.VMEM((CHUNKS * piece, lags), F32),
                pltpu.SemaphoreType.DMA,
                pltpu.VMEM((rows, QUAD * width), BF16),
                pltpu.VMEM((rows, QUAD * width), BF16),
                pltpu.SemaphoreType.DMA((2, QUAD * pieces[0])),
            ],
            input_output_aliases={3 + QUAD + len(last) + n: n for n in range(len(results))},
            compiler_params=PARAMS,
            name=f"gate_products_{chunk}",
        )(pos, key_branch, value_branch, *gradients, *last, *results)
    key_grad, value_grad, filter_grad = results
    return (ungrouped(key_grad), ungrouped(value_grad), filter_grad)


def solution(mesh):
    in_specs = (
        P(("groups", "ctx"), None),
        P(("groups", "ctx"), None),
        P(("groups", "ctx"), None),
        P(("groups", "ctx"), None),
        P("ctx", None),
        P("groups"),
    )
    out_specs = (P(("groups", "ctx"), None), P(("groups", "ctx"), None), P(("groups", "ctx"), None))
    return jax.shard_map(shards, mesh=mesh, in_specs=in_specs, out_specs=out_specs, check_vma=False)
```

```python
import math
from functools import partial

import jax
import jax.numpy as jnp
import ml_dtypes
import numpy as np
from jax import lax
from jax.experimental import pallas as pl
from jax.experimental.pallas import tpu as pltpu
from jax.sharding import PartitionSpec as P

QUAD = 4
CHUNKS = 2
REACH = 2
TILE = 256
F32 = jnp.float32
BF16 = jnp.bfloat16
SMEM = pl.BlockSpec(memory_space=pltpu.SMEM)
VMEM = pl.BlockSpec(memory_space=pltpu.VMEM)
HBM = pl.BlockSpec(memory_space=pltpu.HBM)
ANY = pl.BlockSpec(memory_space=pl.ANY)
PARAMS = pltpu.CompilerParams(vmem_limit_bytes=40 * 1024 * 1024)


def halving_order(count):
    order = [0]
    while len(order) < count:
        order = [2 * n for n in order] + [2 * n + 1 for n in order]
    return order


def split_bf16(table):
    high = table.astype(ml_dtypes.bfloat16)
    low = (table - high.astype(np.float64)).astype(ml_dtypes.bfloat16)
    return high, low


def tables(rows):
    length = 2 * rows
    omega = 2.0 * math.pi * (np.arange(rows) + 0.5) / length
    angle = omega[:, None] * np.arange(length)[None, :]
    forward = np.concatenate([np.cos(angle), -np.sin(angle)], axis=0)
    high, low = split_bf16(forward)
    half = np.concatenate([high[:, :rows], low[:, :rows]], axis=1)
    back_high, back_low = split_bf16(forward[:, :rows].T / rows)
    back = np.concatenate([back_high, back_low], axis=0)
    return np.concatenate([high, low, half, back], axis=0)


def dot(left, right):
    return jnp.dot(left, right, preferred_element_type=F32)


def conj_product(left, right):
    (lr, li), (rr, ri) = left, right
    return lr * rr + li * ri, li * rr - lr * ri


def halves(spectrum):
    rows = spectrum.shape[0] // 2
    return spectrum[:rows], spectrum[rows:]


def add(left, right):
    return left[0] + right[0], left[1] + right[1]


def invert(back, real, imag):
    rows = real.shape[0]
    spectrum = jnp.concatenate([real, imag], axis=0)
    both = dot(back, spectrum.astype(BF16))
    return both[:rows] + both[rows:]


def cut_products(pieces, offset, sources, held, sems, outs):
    count, width = pieces
    section = held[0].shape[1] // count
    copies = []
    for i in range(count):
        lanes = pl.ds(i * section, section)
        for n, (source, target) in enumerate(zip(sources, held)):
            copies.append(pltpu.make_async_copy(source.at[:, lanes], target.at[:, lanes], sems.at[n, i]))
            copies[-1].start()
    for i in range(count):
        copies[2 * i].wait()
        copies[2 * i + 1].wait()
        for out, side, pair, chunks in outs:
            for n, chunk in enumerate(chunks):
                lanes = pl.ds(pl.multiple_of(offset(chunk, i, pair, side), 128), width)
                first = (n * count + i) * width
                out[:, first : first + width] = held[0][:, lanes] * held[1][:, lanes]


def grad_kernel(pieces, offset, pos_ref, left_hbm, right_hbm, own, near, same, other, left_ref, right_ref, sems):
    place = pos_ref[0] % QUAD
    core, chip = place % 2, place // 2
    every = range(CHUNKS)
    outs = [(same, core, 1 - chip, every), (other, 1 - core, 1 - chip, every)]
    outs += [(near, 1 - core, chip, every), (own, core, chip, every)]
    cut_products(pieces, offset, (left_hbm, right_hbm), (left_ref, right_ref), sems, outs)


def input_kernel(pieces, offset, pos_ref, left_hbm, right_hbm, _, own, near, *refs):
    far, (left_ref, right_ref, sems) = refs[:-3], refs[-3:]
    rows = own.shape[0]
    place = pos_ref[0] % QUAD
    core, chip = place % 2, place // 2
    outs = [(near, 1 - core, chip, range(CHUNKS)), (own, core, chip, range(CHUNKS))]
    for chunk, out in enumerate(far):
        outs += [(out.at[:rows, :], core, 1 - chip, [chunk]), (out.at[rows:, :], 1 - core, 1 - chip, [chunk])]
    cut_products(pieces, offset, (left_hbm, right_hbm), (left_ref, right_ref), sems, outs)


def pack_kernel(chunk, near_ref, came_ref, *refs):
    out = refs[-1]
    rows, width = near_ref.shape[0], out.shape[1]
    out[:rows, :] = near_ref[:, chunk * width : (chunk + 1) * width]
    out[rows:, :] = came_ref[rows:, :]


def filter_kernel(quads, pos_ref, table_ref, *refs):
    parts, out, taps_all = refs[:-2], refs[-2], refs[-1]
    quad = pos_ref[0] // QUAD
    channels, lags = taps_all.shape
    rows = lags // REACH
    half = table_ref[2 * lags : 3 * lags]
    width = channels // CHUNKS
    piece = width // quads
    held = [(part, at) for part in parts for at in range(0, part.shape[0], CHUNKS * piece)]
    for s, (part, first) in zip(halving_order(quads), held):
        for chunk in range(CHUNKS):
            at = pl.ds(pl.multiple_of(chunk * width + lax.bitwise_xor(quad, s) * piece, piece), piece)
            taps_all[at, :] = part[first + chunk * piece : first + (chunk + 1) * piece, :]
    for first in range(0, channels, TILE):
        for segment in range(REACH):
            taps = taps_all[first : first + TILE, segment * rows : (segment + 1) * rows]
            twice = jnp.concatenate([taps, taps], axis=1)
            spectrum = lax.dot_general(half, twice, (((1,), (1,)), ((), ())), preferred_element_type=F32)
            out[segment * lags : (segment + 1) * lags, first : first + TILE] = spectrum


def gate_kernel(*refs):
    del refs


def halo_kernel(chunks, pos_ref, *refs):
    place = pos_ref[0] % QUAD
    held, outs = refs[:QUAD], refs[-chunks:]
    rows, width = held[0].shape[0], outs[0].shape[1]
    for block in range(REACH):
        for k in range(QUAD):

            @pl.when(lax.bitwise_xor(place, k) == block)
            def _():
                for chunk, out in enumerate(outs):
                    out[block * rows : (block + 1) * rows, :] = held[k][:rows, chunk * width : (chunk + 1) * width]


def joined_blocks(pos_ref, docs_ref, docs):
    joined = []
    for j in range(QUAD + 1):
        same, end = jnp.int32(1), jnp.int32(0)
        for d in range(docs):
            end = end + docs_ref[d]
            same = jnp.where(end == pos_ref[0] // QUAD * QUAD + j + 1, 0, same)
        joined.append(same.astype(F32))
    return joined


def convolve(joined, table_ref, filters, grad_of, input_of, put):
    length = table_ref.shape[1]
    half, back = table_ref[2 * length : 3 * length], table_ref[3 * length :]
    windows = []
    for j in range(QUAD + 1):
        both = jnp.concatenate([grad_of(j), grad_of(j + 1) * joined[j].astype(BF16)], axis=0)
        parts = dot(table_ref[: 2 * length], both)
        windows.append(parts[:length] + parts[length:])
    sources = [halves(dot(half, jnp.concatenate([input_of(j)] * 2, axis=0))) for j in range(QUAD)]
    sums = None
    for j in range(QUAD):
        near, far = halves(windows[j]), halves(windows[j + 1] * joined[j])
        real, imag = add(conj_product(near, filters[0]), conj_product(far, filters[1]))
        put(j, invert(back, real, imag).astype(BF16))
        terms = [conj_product(near, sources[j]), conj_product(far, sources[j])]
        sums = [add(*pair) for pair in zip(sums, terms)] if sums else terms
    return sums


def tiles(width):
    return [slice(first, min(first + TILE, width)) for first in range(0, width, TILE)]


def conv_kernel(chunk, quads, docs, pos_ref, docs_ref, table_ref, filter_ref, halo_ref, *refs):
    grads, (own_ref, far_ref, came_ref) = refs[:QUAD], refs[QUAD : QUAD + 3]
    outs, terms = refs[-6 - QUAD : -6], refs[-6:-4]
    grad_all, input_all, out_all, terms_all = refs[-4:]
    rows, width = outs[0].shape
    length = 2 * rows
    piece = width // quads
    place, quad = pos_ref[0] % QUAD, pos_ref[0] // QUAD
    share = slice(chunk * width, (chunk + 1) * width)
    joined = joined_blocks(pos_ref, docs_ref, docs)
    for k in range(QUAD):
        at = pl.ds(pl.multiple_of(lax.bitwise_xor(place, k) * rows, rows), rows)
        grad_all[at, :] = grads[k][:, share]
        if k:
            held = (far_ref if k == 2 else came_ref)[k // 3 * rows : (k // 3 + 1) * rows, :]
        else:
            held = own_ref[:, share]
        input_all[at, :] = held
    grad_all[QUAD * rows :, :] = halo_ref[...]
    for lanes in tiles(width):

        def put(j, value, lanes=lanes):
            out_all[j * rows : (j + 1) * rows, lanes] = value

        of_chunk = slice(chunk * width + lanes.start, chunk * width + lanes.stop)
        filters = [halves(filter_ref[n * length : (n + 1) * length, of_chunk]) for n in range(REACH)]
        block = lambda ref, j, lanes=lanes: ref[j * rows : (j + 1) * rows, lanes]
        sums = convolve(joined, table_ref, filters, partial(block, grad_all), partial(block, input_all), put)
        for segment in range(REACH):
            lags = invert(table_ref[3 * length :], *sums[segment])
            terms_all[lanes, segment * rows : (segment + 1) * rows] = lags.T
    for k in range(QUAD):
        at = pl.ds(pl.multiple_of(lax.bitwise_xor(place, k) * rows, rows), rows)
        if k == 1 and chunk:
            outs[k][:, : chunk * width] = refs[QUAD + 3][...]
            outs[k][:, chunk * width :] = out_all[at, :]
        else:
            outs[k][...] = out_all[at, :]
    for n, s in enumerate(halving_order(quads)):
        at = pl.ds(pl.multiple_of(lax.bitwise_xor(quad, s) * piece, piece), piece)
        sent, n = divmod(n, quads // 2)
        terms[sent][n * piece : (n + 1) * piece, :] = terms_all[at, :].astype(terms[sent].dtype)


def fold_kernel(kept_ref, came_ref, keep_ref, send_ref):
    half = keep_ref.shape[0]
    keep_ref[...] = kept_ref[:half, :] + came_ref[:half, :].astype(F32)
    send_ref[...] = (kept_ref[half:, :] + came_ref[half:, :].astype(F32)).astype(BF16)


def final_kernel(chunk, pieces, offset, scale, terms, pos_ref, key_ref, value_ref, *refs):
    grads, filters = refs[:QUAD], refs[QUAD : QUAD + terms]
    filter_all, filter_sem, key_all, value_all, sems = refs[-5:]
    key_out, value_out, *filter_out = refs[-8 if terms else -7 : -5]
    place = pos_ref[0] % QUAD
    count, width = pieces
    copies = []
    for n in range(terms // 2):
        kept, came = filters[2 * n], filters[2 * n + 1]
        rows = kept.shape[0]
        filter_all[n * rows : (n + 1) * rows, :] = (kept[...] + came[...].astype(F32)) * scale
    for out in filter_out:
        copies.append(pltpu.make_async_copy(filter_all, out, filter_sem))
        copies[-1].start()
    for k in range(QUAD):
        member = lax.bitwise_xor(place, k)
        for i in range(count):
            n = k * count + i
            lanes = pl.ds(pl.multiple_of(offset(chunk, i, member // 2, member % 2), 128), width)
            held = slice(n * width, (n + 1) * width)
            first = ((chunk * count if k == 1 else 0) + i) * width
            grad = grads[k][:, first : first + width]
            key_all[:, held] = grad * value_ref[:, lanes]
            value_all[:, held] = grad * key_ref[:, lanes]
            copies.append(pltpu.make_async_copy(key_all.at[:, held], key_out.at[:, lanes], sems.at[0, n]))
            copies.append(pltpu.make_async_copy(value_all.at[:, held], value_out.at[:, lanes], sems.at[1, n]))
            copies[-2].start()
            copies[-1].start()
    for copy in copies:
        copy.wait()


def shards(query_gate, key_branch, value_branch, out_grad, filter_taps, doc_blocks):
    blocks = lax.axis_size("ctx")
    quads = blocks // QUAD
    rows, channels = query_gate.shape
    lags = filter_taps.shape[1]
    piece = channels // (QUAD * quads * CHUNKS)
    width = quads * piece
    pos = lax.axis_index("ctx").astype(jnp.int32).reshape(1)
    table = jnp.asarray(tables(rows))
    aligned = piece % 128 == 0

    def grouped(array):
        if aligned:
            return array
        parts = array.reshape(rows, quads, QUAD, CHUNKS, piece)
        return parts.transpose(0, 2, 3, 1, 4).reshape(rows, channels)

    def ungrouped(array):
        if aligned:
            return array
        parts = array.reshape(rows, QUAD, CHUNKS, quads, piece)
        return parts.transpose(0, 3, 1, 2, 4).reshape(rows, channels)

    if aligned:
        pieces = (quads, piece)
        offset = lambda chunk, i, pair, side: (((2 * i + pair) * 2 + side) * CHUNKS + chunk) * piece
    else:
        pieces = (1, width)
        offset = lambda chunk, i, pair, side: ((2 * pair + side) * CHUNKS + chunk) * width

    def to_member(value, k):
        return lax.ppermute(value, "ctx", [(i, i ^ k) for i in range(blocks)]) if k else value

    def gate(values, *after):
        return pl.pallas_call(
            gate_kernel,
            out_shape=[jax.ShapeDtypeStruct(value.shape, value.dtype) for value in values],
            in_specs=[ANY] * (len(values) + len(after)),
            out_specs=[ANY] * len(values),
            input_output_aliases={n: n for n in range(len(values))},
            compiler_params=PARAMS,
            name="gate",
        )(*values, *after)

    def to_quad(value, s):
        return to_member(value, QUAD * s)

    key_branch, value_branch = grouped(key_branch), grouped(value_branch)
    out_grad, query_gate = grouped(out_grad), grouped(query_gate)
    parts, step = [filter_taps], quads // 2
    while step > 1:
        held = parts[0] if len(parts) == 1 else jnp.concatenate(parts, axis=0)
        parts, step = [held, to_quad(held, step)], step // 2
    if quads > 1:
        first = to_quad(parts[0], 1)
        parts += [first, *[to_quad(gate([part], first)[0], 1) for part in parts[1:]]]

    alone, both = jax.ShapeDtypeStruct((rows, width), BF16), jax.ShapeDtypeStruct((rows, CHUNKS * width), BF16)
    def products(kernel, left, right, types, limit, name, *after):
        return pl.pallas_call(
            partial(kernel, pieces, offset),
            out_shape=types,
            in_specs=[SMEM] + [HBM] * 2 + [ANY] * len(after),
            out_specs=[VMEM] * len(types),
            scratch_shapes=[pltpu.VMEM((rows, channels), BF16)] * 2 + [pltpu.SemaphoreType.DMA((2, pieces[0]))],
            compiler_params=pltpu.CompilerParams(vmem_limit_bytes=limit * 1024 * 1024),
            name=name,
        )(pos, left, right, *after)

    own, near, same, other = products(grad_kernel, out_grad, query_gate, [both] * 4, 60, "gated_grad")
    grads = [own, to_member(near, 1), to_member(same, 2), to_member(other, 3)]
    pair_type = jax.ShapeDtypeStruct((2 * rows, width), BF16)
    own, near, *far_inputs = products(input_kernel, key_branch, value_branch, [both] * 2 + [pair_type] * CHUNKS, 40, "conv_input", grads[1])
    own_input, near_input = own, near
    far_inputs[0] = to_member(far_inputs[0], 2)
    far_inputs[1] = to_member(gate([far_inputs[1]], far_inputs[0])[0], 2)
    spectra = pl.pallas_call(
        partial(filter_kernel, quads),
        out_shape=jax.ShapeDtypeStruct((REACH * lags, CHUNKS * width), F32),
        in_specs=[SMEM, VMEM] + [VMEM] * len(parts),
        out_specs=VMEM,
        scratch_shapes=[pltpu.VMEM((CHUNKS * width, lags), BF16)],
        compiler_params=PARAMS,
        name="filter_spectra",
    )(pos, table, *parts)
    first_blocks = pl.pallas_call(
        partial(halo_kernel, CHUNKS),
        out_shape=[jax.ShapeDtypeStruct((REACH * rows, width), BF16)] * CHUNKS,
        in_specs=[SMEM] + [VMEM] * QUAD,
        out_specs=[VMEM] * CHUNKS,
        compiler_params=PARAMS,
        name="halo",
    )(pos, *grads)
    before = [first_blocks[0], spectra]
    results, chunk_grads, chunk_terms = [], [], []
    nearest = []
    for chunk in range(CHUNKS):
        halo = lax.ppermute(first_blocks[chunk], "ctx", [(i, i - QUAD) for i in range(QUAD, blocks)])
        forward = pl.pallas_call(
            partial(pack_kernel, chunk),
            out_shape=pair_type,
            in_specs=[VMEM, VMEM] + [ANY] * len(before),
            out_specs=VMEM,
            compiler_params=PARAMS,
            name=f"pack_{chunk}",
        )(near_input, far_inputs[chunk], *before)
        forward = to_member(forward, 1)
        done = pl.pallas_call(
            partial(conv_kernel, chunk, quads, doc_blocks.shape[0]),
            out_shape=[alone, jax.ShapeDtypeStruct((rows, (chunk + 1) * width), BF16), alone, alone]
            + [jax.ShapeDtypeStruct((width // 2, lags), kind) for kind in (F32, BF16)],
            in_specs=[SMEM, SMEM] + [VMEM] * (6 + QUAD + len(nearest)),
            out_specs=[VMEM] * (QUAD + 2),
            scratch_shapes=[
                pltpu.VMEM(((QUAD + REACH) * rows, width), BF16),
                pltpu.VMEM((QUAD * rows, width), BF16),
                pltpu.VMEM((QUAD * rows, width), BF16),
                pltpu.VMEM((width, lags), F32),
            ],
            compiler_params=PARAMS,
            name=f"conv_{chunk}",
        )(pos, doc_blocks, table, spectra, halo, *grads, own_input, far_inputs[chunk], forward, *nearest)
        own, pair, *sent, kept, send = done
        before, nearest = [pair], [pair]
        if chunk:
            *sent, pair, send = gate([*sent, pair, send], *chunk_grads[-1][2:], chunk_terms[-1][1])
        chunk_grads.append([own, pair, *[to_member(value, 2 + k) for k, value in enumerate(sent)]])
        chunk_terms.append((kept, to_quad(send, 1)))
    nearest = to_member(pair, 1)
    filter_grads = []
    for chunk in range(CHUNKS):
        gradients, (kept, came) = chunk_grads[chunk], chunk_terms[chunk]
        gradients[1] = nearest
        step = 1
        while 2 * step < quads:
            step *= 2
            half = kept.shape[0] // 2
            kept, send = pl.pallas_call(
                fold_kernel,
                out_shape=[jax.ShapeDtypeStruct((half, lags), kind) for kind in (F32, BF16)],
                in_specs=[VMEM] * 2,
                out_specs=[VMEM] * 2,
                compiler_params=PARAMS,
                name=f"fold_{chunk}_{step}",
            )(kept, came)
            came = to_quad(send, step)
        filter_grads += [kept, came]
        last = filter_grads if chunk == CHUNKS - 1 else []
        results = pl.pallas_call(
            partial(final_kernel, chunk, pieces, offset, 1.0 / math.sqrt(rows * blocks), len(last)),
            out_shape=[jax.ShapeDtypeStruct((rows, channels), BF16)] * 2
            + [jax.ShapeDtypeStruct((CHUNKS * piece, lags), F32)] * (len(last) > 0),
            in_specs=[SMEM] + [VMEM] * (2 + QUAD + len(last)) + [HBM] * len(results),
            out_specs=[HBM] * (3 if last else 2),
            scratch_shapes=[
                pltpu.VMEM((CHUNKS * piece, lags), F32),
                pltpu.SemaphoreType.DMA,
                pltpu.VMEM((rows, QUAD * width), BF16),
                pltpu.VMEM((rows, QUAD * width), BF16),
                pltpu.SemaphoreType.DMA((2, QUAD * pieces[0])),
            ],
            input_output_aliases={3 + QUAD + len(last) + n: n for n in range(len(results))},
            compiler_params=PARAMS,
            name=f"gate_products_{chunk}",
        )(pos, key_branch, value_branch, *gradients, *last, *results)
    key_grad, value_grad, filter_grad = results
    return (ungrouped(key_grad), ungrouped(value_grad), filter_grad)


def solution(mesh):
    in_specs = (
        P(("groups", "ctx"), None),
        P(("groups", "ctx"), None),
        P(("groups", "ctx"), None),
        P(("groups", "ctx"), None),
        P("ctx", None),
        P("groups"),
    )
    out_specs = (P(("groups", "ctx"), None), P(("groups", "ctx"), None), P(("groups", "ctx"), None))
    return jax.shard_map(shards, mesh=mesh, in_specs=in_specs, out_specs=out_specs, check_vma=False)
```

```python
import math
from functools import partial

import jax
import jax.numpy as jnp
import ml_dtypes
import numpy as np
from jax import lax
from jax.experimental import pallas as pl
from jax.experimental.pallas import tpu as pltpu
from jax.sharding import PartitionSpec as P

QUAD = 4
CHUNKS = 2
REACH = 2
TILE = 256
F32 = jnp.float32
BF16 = jnp.bfloat16
SMEM = pl.BlockSpec(memory_space=pltpu.SMEM)
VMEM = pl.BlockSpec(memory_space=pltpu.VMEM)
HBM = pl.BlockSpec(memory_space=pltpu.HBM)
ANY = pl.BlockSpec(memory_space=pl.ANY)
PARAMS = pltpu.CompilerParams(vmem_limit_bytes=40 * 1024 * 1024)


def halving_order(count):
    order = [0]
    while len(order) < count:
        order = [2 * n for n in order] + [2 * n + 1 for n in order]
    return order


def split_bf16(table):
    high = table.astype(ml_dtypes.bfloat16)
    low = (table - high.astype(np.float64)).astype(ml_dtypes.bfloat16)
    return high, low


def tables(rows):
    length = 2 * rows
    omega = 2.0 * math.pi * (np.arange(rows) + 0.5) / length
    angle = omega[:, None] * np.arange(length)[None, :]
    forward = np.concatenate([np.cos(angle), -np.sin(angle)], axis=0)
    high, low = split_bf16(forward)
    half = np.concatenate([high[:, :rows], low[:, :rows]], axis=1)
    back_high, back_low = split_bf16(forward[:, :rows].T / rows)
    back = np.concatenate([back_high, back_low], axis=0)
    return np.concatenate([high, low, half, back], axis=0)


def dot(left, right):
    return jnp.dot(left, right, preferred_element_type=F32)


def conj_product(left, right):
    (lr, li), (rr, ri) = left, right
    return lr * rr + li * ri, li * rr - lr * ri


def halves(spectrum):
    rows = spectrum.shape[0] // 2
    return spectrum[:rows], spectrum[rows:]


def add(left, right):
    return left[0] + right[0], left[1] + right[1]


def invert(back, real, imag):
    rows = real.shape[0]
    spectrum = jnp.concatenate([real, imag], axis=0)
    both = dot(back, spectrum.astype(BF16))
    return both[:rows] + both[rows:]


def cut_products(pieces, offset, sources, held, sems, outs):
    count, width = pieces
    section = held[0].shape[1] // count
    copies = []
    for i in range(count):
        lanes = pl.ds(i * section, section)
        for n, (source, target) in enumerate(zip(sources, held)):
            copies.append(pltpu.make_async_copy(source.at[:, lanes], target.at[:, lanes], sems.at[n, i]))
            copies[-1].start()
    for i in range(count):
        copies[2 * i].wait()
        copies[2 * i + 1].wait()
        for out, side, pair, chunks in outs:
            for n, chunk in enumerate(chunks):
                lanes = pl.ds(pl.multiple_of(offset(chunk, i, pair, side), 128), width)
                first = (n * count + i) * width
                out[:, first : first + width] = held[0][:, lanes] * held[1][:, lanes]


def grad_kernel(pieces, offset, pos_ref, left_hbm, right_hbm, own, near, same, other, left_ref, right_ref, sems):
    place = pos_ref[0] % QUAD
    core, chip = place % 2, place // 2
    every = range(CHUNKS)
    outs = [(same, core, 1 - chip, every), (other, 1 - core, 1 - chip, every)]
    outs += [(near, 1 - core, chip, every), (own, core, chip, every)]
    cut_products(pieces, offset, (left_hbm, right_hbm), (left_ref, right_ref), sems, outs)


def input_kernel(pieces, offset, pos_ref, left_hbm, right_hbm, _, own, near, *refs):
    far, (left_ref, right_ref, sems) = refs[:-3], refs[-3:]
    rows = own.shape[0]
    place = pos_ref[0] % QUAD
    core, chip = place % 2, place // 2
    outs = [(near, 1 - core, chip, range(CHUNKS)), (own, core, chip, range(CHUNKS))]
    for chunk, out in enumerate(far):
        outs += [(out.at[:rows, :], core, 1 - chip, [chunk]), (out.at[rows:, :], 1 - core, 1 - chip, [chunk])]
    cut_products(pieces, offset, (left_hbm, right_hbm), (left_ref, right_ref), sems, outs)


def pack_kernel(chunk, near_ref, came_ref, *refs):
    out = refs[-1]
    rows, width = near_ref.shape[0], out.shape[1]
    out[:rows, :] = near_ref[:, chunk * width : (chunk + 1) * width]
    out[rows:, :] = came_ref[rows:, :]


def filter_kernel(quads, pos_ref, table_ref, *refs):
    parts, out, taps_all = refs[:-2], refs[-2], refs[-1]
    quad = pos_ref[0] // QUAD
    channels, lags = taps_all.shape
    rows = lags // REACH
    half = table_ref[2 * lags : 3 * lags]
    width = channels // CHUNKS
    piece = width // quads
    held = [(part, at) for part in parts for at in range(0, part.shape[0], CHUNKS * piece)]
    for s, (part, first) in zip(halving_order(quads), held):
        for chunk in range(CHUNKS):
            at = pl.ds(pl.multiple_of(chunk * width + lax.bitwise_xor(quad, s) * piece, piece), piece)
            taps_all[at, :] = part[first + chunk * piece : first + (chunk + 1) * piece, :]
    for first in range(0, channels, TILE):
        for segment in range(REACH):
            taps = taps_all[first : first + TILE, segment * rows : (segment + 1) * rows]
            twice = jnp.concatenate([taps, taps], axis=1)
            spectrum = lax.dot_general(half, twice, (((1,), (1,)), ((), ())), preferred_element_type=F32)
            out[segment * lags : (segment + 1) * lags, first : first + TILE] = spectrum


def gate_kernel(*refs):
    del refs


def halo_kernel(chunks, pos_ref, *refs):
    place = pos_ref[0] % QUAD
    held, outs = refs[:QUAD], refs[-chunks:]
    rows, width = held[0].shape[0], outs[0].shape[1]
    for block in range(REACH):
        for k in range(QUAD):

            @pl.when(lax.bitwise_xor(place, k) == block)
            def _():
                for chunk, out in enumerate(outs):
                    out[block * rows : (block + 1) * rows, :] = held[k][:rows, chunk * width : (chunk + 1) * width]


def joined_blocks(pos_ref, docs_ref, docs):
    joined = []
    for j in range(QUAD + 1):
        same, end = jnp.int32(1), jnp.int32(0)
        for d in range(docs):
            end = end + docs_ref[d]
            same = jnp.where(end == pos_ref[0] // QUAD * QUAD + j + 1, 0, same)
        joined.append(same.astype(F32))
    return joined


def convolve(joined, table_ref, filters, grad_of, input_of, put):
    length = table_ref.shape[1]
    half, back = table_ref[2 * length : 3 * length], table_ref[3 * length :]
    windows = []
    for j in range(QUAD + 1):
        both = jnp.concatenate([grad_of(j), grad_of(j + 1) * joined[j].astype(BF16)], axis=0)
        parts = dot(table_ref[: 2 * length], both)
        windows.append(parts[:length] + parts[length:])
    sources = [halves(dot(half, jnp.concatenate([input_of(j)] * 2, axis=0))) for j in range(QUAD)]
    sums = None
    for j in range(QUAD):
        near, far = halves(windows[j]), halves(windows[j + 1] * joined[j])
        real, imag = add(conj_product(near, filters[0]), conj_product(far, filters[1]))
        put(j, invert(back, real, imag).astype(BF16))
        terms = [conj_product(near, sources[j]), conj_product(far, sources[j])]
        sums = [add(*pair) for pair in zip(sums, terms)] if sums else terms
    return sums


def tiles(width):
    return [slice(first, min(first + TILE, width)) for first in range(0, width, TILE)]


def conv_kernel(chunk, quads, docs, pos_ref, docs_ref, table_ref, filter_ref, halo_ref, *refs):
    grads, (own_ref, far_ref, came_ref) = refs[:QUAD], refs[QUAD : QUAD + 3]
    outs, terms = refs[-6 - QUAD : -6], refs[-6:-4]
    grad_all, input_all, out_all, terms_all = refs[-4:]
    rows, width = outs[0].shape
    length = 2 * rows
    piece = width // quads
    place, quad = pos_ref[0] % QUAD, pos_ref[0] // QUAD
    share = slice(chunk * width, (chunk + 1) * width)
    joined = joined_blocks(pos_ref, docs_ref, docs)
    for k in range(QUAD):
        at = pl.ds(pl.multiple_of(lax.bitwise_xor(place, k) * rows, rows), rows)
        grad_all[at, :] = grads[k][:, share]
        if k:
            held = (far_ref if k == 2 else came_ref)[k // 3 * rows : (k // 3 + 1) * rows, :]
        else:
            held = own_ref[:, share]
        input_all[at, :] = held
    grad_all[QUAD * rows :, :] = halo_ref[...]
    for lanes in tiles(width):

        def put(j, value, lanes=lanes):
            out_all[j * rows : (j + 1) * rows, lanes] = value

        of_chunk = slice(chunk * width + lanes.start, chunk * width + lanes.stop)
        filters = [halves(filter_ref[n * length : (n + 1) * length, of_chunk]) for n in range(REACH)]
        block = lambda ref, j, lanes=lanes: ref[j * rows : (j + 1) * rows, lanes]
        sums = convolve(joined, table_ref, filters, partial(block, grad_all), partial(block, input_all), put)
        for segment in range(REACH):
            spectrum = jnp.concatenate(sums[segment], axis=0).astype(BF16)
            both = lax.dot_general(spectrum, table_ref[3 * length :], (((0,), (1,)), ((), ())), preferred_element_type=F32)
            terms_all[lanes, segment * rows : (segment + 1) * rows] = both[:, :rows] + both[:, rows:]
    for k in range(QUAD):
        at = pl.ds(pl.multiple_of(lax.bitwise_xor(place, k) * rows, rows), rows)
        if k == 1 and chunk:
            outs[k][:, : chunk * width] = refs[QUAD + 3][...]
            outs[k][:, chunk * width :] = out_all[at, :]
        else:
            outs[k][...] = out_all[at, :]
    for n, s in enumerate(halving_order(quads)):
        at = pl.ds(pl.multiple_of(lax.bitwise_xor(quad, s) * piece, piece), piece)
        sent, n = divmod(n, quads // 2)
        terms[sent][n * piece : (n + 1) * piece, :] = terms_all[at, :].astype(terms[sent].dtype)


def fold_kernel(kept_ref, came_ref, keep_ref, send_ref):
    half = keep_ref.shape[0]
    keep_ref[...] = kept_ref[:half, :] + came_ref[:half, :].astype(F32)
    send_ref[...] = (kept_ref[half:, :] + came_ref[half:, :].astype(F32)).astype(BF16)


def final_kernel(chunk, pieces, offset, scale, terms, pos_ref, key_ref, value_ref, *refs):
    grads, filters = refs[:QUAD], refs[QUAD : QUAD + terms]
    filter_all, filter_sem, key_all, value_all, sems = refs[-5:]
    key_out, value_out, *filter_out = refs[-8 if terms else -7 : -5]
    place = pos_ref[0] % QUAD
    count, width = pieces
    copies = []
    for n in range(terms // 2):
        kept, came = filters[2 * n], filters[2 * n + 1]
        rows = kept.shape[0]
        filter_all[n * rows : (n + 1) * rows, :] = (kept[...] + came[...].astype(F32)) * scale
    for out in filter_out:
        copies.append(pltpu.make_async_copy(filter_all, out, filter_sem))
        copies[-1].start()
    for k in range(QUAD):
        member = lax.bitwise_xor(place, k)
        for i in range(count):
            n = k * count + i
            lanes = pl.ds(pl.multiple_of(offset(chunk, i, member // 2, member % 2), 128), width)
            held = slice(n * width, (n + 1) * width)
            first = ((chunk * count if k == 1 else 0) + i) * width
            grad = grads[k][:, first : first + width]
            key_all[:, held] = grad * value_ref[:, lanes]
            value_all[:, held] = grad * key_ref[:, lanes]
            copies.append(pltpu.make_async_copy(key_all.at[:, held], key_out.at[:, lanes], sems.at[0, n]))
            copies.append(pltpu.make_async_copy(value_all.at[:, held], value_out.at[:, lanes], sems.at[1, n]))
            copies[-2].start()
            copies[-1].start()
    for copy in copies:
        copy.wait()


def shards(query_gate, key_branch, value_branch, out_grad, filter_taps, doc_blocks):
    blocks = lax.axis_size("ctx")
    quads = blocks // QUAD
    rows, channels = query_gate.shape
    lags = filter_taps.shape[1]
    piece = channels // (QUAD * quads * CHUNKS)
    width = quads * piece
    pos = lax.axis_index("ctx").astype(jnp.int32).reshape(1)
    table = jnp.asarray(tables(rows))
    aligned = piece % 128 == 0

    def grouped(array):
        if aligned:
            return array
        parts = array.reshape(rows, quads, QUAD, CHUNKS, piece)
        return parts.transpose(0, 2, 3, 1, 4).reshape(rows, channels)

    def ungrouped(array):
        if aligned:
            return array
        parts = array.reshape(rows, QUAD, CHUNKS, quads, piece)
        return parts.transpose(0, 3, 1, 2, 4).reshape(rows, channels)

    if aligned:
        pieces = (quads, piece)
        offset = lambda chunk, i, pair, side: (((2 * i + pair) * 2 + side) * CHUNKS + chunk) * piece
    else:
        pieces = (1, width)
        offset = lambda chunk, i, pair, side: ((2 * pair + side) * CHUNKS + chunk) * width

    def to_member(value, k):
        return lax.ppermute(value, "ctx", [(i, i ^ k) for i in range(blocks)]) if k else value

    def gate(values, *after):
        return pl.pallas_call(
            gate_kernel,
            out_shape=[jax.ShapeDtypeStruct(value.shape, value.dtype) for value in values],
            in_specs=[ANY] * (len(values) + len(after)),
            out_specs=[ANY] * len(values),
            input_output_aliases={n: n for n in range(len(values))},
            compiler_params=PARAMS,
            name="gate",
        )(*values, *after)

    def to_quad(value, s):
        return to_member(value, QUAD * s)

    key_branch, value_branch = grouped(key_branch), grouped(value_branch)
    out_grad, query_gate = grouped(out_grad), grouped(query_gate)
    parts, step = [filter_taps], quads // 2
    while step > 1:
        held = parts[0] if len(parts) == 1 else jnp.concatenate(parts, axis=0)
        parts, step = [held, to_quad(held, step)], step // 2
    if quads > 1:
        first = to_quad(parts[0], 1)
        parts += [first, *[to_quad(gate([part], first)[0], 1) for part in parts[1:]]]

    alone, both = jax.ShapeDtypeStruct((rows, width), BF16), jax.ShapeDtypeStruct((rows, CHUNKS * width), BF16)
    def products(kernel, left, right, types, limit, name, *after):
        return pl.pallas_call(
            partial(kernel, pieces, offset),
            out_shape=types,
            in_specs=[SMEM] + [HBM] * 2 + [ANY] * len(after),
            out_specs=[VMEM] * len(types),
            scratch_shapes=[pltpu.VMEM((rows, channels), BF16)] * 2 + [pltpu.SemaphoreType.DMA((2, pieces[0]))],
            compiler_params=pltpu.CompilerParams(vmem_limit_bytes=limit * 1024 * 1024),
            name=name,
        )(pos, left, right, *after)

    own, near, same, other = products(grad_kernel, out_grad, query_gate, [both] * 4, 60, "gated_grad")
    grads = [own, to_member(near, 1), to_member(same, 2), to_member(other, 3)]
    pair_type = jax.ShapeDtypeStruct((2 * rows, width), BF16)
    own, near, *far_inputs = products(input_kernel, key_branch, value_branch, [both] * 2 + [pair_type] * CHUNKS, 40, "conv_input", grads[1])
    own_input, near_input = own, near
    far_inputs[0] = to_member(far_inputs[0], 2)
    far_inputs[1] = to_member(gate([far_inputs[1]], far_inputs[0])[0], 2)
    spectra = pl.pallas_call(
        partial(filter_kernel, quads),
        out_shape=jax.ShapeDtypeStruct((REACH * lags, CHUNKS * width), F32),
        in_specs=[SMEM, VMEM] + [VMEM] * len(parts),
        out_specs=VMEM,
        scratch_shapes=[pltpu.VMEM((CHUNKS * width, lags), BF16)],
        compiler_params=PARAMS,
        name="filter_spectra",
    )(pos, table, *parts)
    first_blocks = pl.pallas_call(
        partial(halo_kernel, CHUNKS),
        out_shape=[jax.ShapeDtypeStruct((REACH * rows, width), BF16)] * CHUNKS,
        in_specs=[SMEM] + [VMEM] * QUAD,
        out_specs=[VMEM] * CHUNKS,
        compiler_params=PARAMS,
        name="halo",
    )(pos, *grads)
    before = [first_blocks[0], spectra]
    results, chunk_grads, chunk_terms = [], [], []
    nearest = []
    for chunk in range(CHUNKS):
        halo = lax.ppermute(first_blocks[chunk], "ctx", [(i, i - QUAD) for i in range(QUAD, blocks)])
        forward = pl.pallas_call(
            partial(pack_kernel, chunk),
            out_shape=pair_type,
            in_specs=[VMEM, VMEM] + [ANY] * len(before),
            out_specs=VMEM,
            compiler_params=PARAMS,
            name=f"pack_{chunk}",
        )(near_input, far_inputs[chunk], *before)
        forward = to_member(forward, 1)
        done = pl.pallas_call(
            partial(conv_kernel, chunk, quads, doc_blocks.shape[0]),
            out_shape=[alone, jax.ShapeDtypeStruct((rows, (chunk + 1) * width), BF16), alone, alone]
            + [jax.ShapeDtypeStruct((width // 2, lags), kind) for kind in (F32, BF16)],
            in_specs=[SMEM, SMEM] + [VMEM] * (6 + QUAD + len(nearest)),
            out_specs=[VMEM] * (QUAD + 2),
            scratch_shapes=[
                pltpu.VMEM(((QUAD + REACH) * rows, width), BF16),
                pltpu.VMEM((QUAD * rows, width), BF16),
                pltpu.VMEM((QUAD * rows, width), BF16),
                pltpu.VMEM((width, lags), F32),
            ],
            compiler_params=PARAMS,
            name=f"conv_{chunk}",
        )(pos, doc_blocks, table, spectra, halo, *grads, own_input, far_inputs[chunk], forward, *nearest)
        own, pair, *sent, kept, send = done
        before, nearest = [pair], [pair]
        if chunk:
            *sent, pair, send = gate([*sent, pair, send], *chunk_grads[-1][2:], chunk_terms[-1][1])
        chunk_grads.append([own, pair, *[to_member(value, 2 + k) for k, value in enumerate(sent)]])
        chunk_terms.append((kept, to_quad(send, 1)))
    nearest = to_member(pair, 1)
    filter_grads = []
    for chunk in range(CHUNKS):
        gradients, (kept, came) = chunk_grads[chunk], chunk_terms[chunk]
        gradients[1] = nearest
        step = 1
        while 2 * step < quads:
            step *= 2
            half = kept.shape[0] // 2
            kept, send = pl.pallas_call(
                fold_kernel,
                out_shape=[jax.ShapeDtypeStruct((half, lags), kind) for kind in (F32, BF16)],
                in_specs=[VMEM] * 2,
                out_specs=[VMEM] * 2,
                compiler_params=PARAMS,
                name=f"fold_{chunk}_{step}",
            )(kept, came)
            came = to_quad(send, step)
        filter_grads += [kept, came]
        last = filter_grads if chunk == CHUNKS - 1 else []
        results = pl.pallas_call(
            partial(final_kernel, chunk, pieces, offset, 1.0 / math.sqrt(rows * blocks), len(last)),
            out_shape=[jax.ShapeDtypeStruct((rows, channels), BF16)] * 2
            + [jax.ShapeDtypeStruct((CHUNKS * piece, lags), F32)] * (len(last) > 0),
            in_specs=[SMEM] + [VMEM] * (2 + QUAD + len(last)) + [HBM] * len(results),
            out_specs=[HBM] * (3 if last else 2),
            scratch_shapes=[
                pltpu.VMEM((CHUNKS * piece, lags), F32),
                pltpu.SemaphoreType.DMA,
                pltpu.VMEM((rows, QUAD * width), BF16),
                pltpu.VMEM((rows, QUAD * width), BF16),
                pltpu.SemaphoreType.DMA((2, QUAD * pieces[0])),
            ],
            input_output_aliases={3 + QUAD + len(last) + n: n for n in range(len(results))},
            compiler_params=PARAMS,
            name=f"gate_products_{chunk}",
        )(pos, key_branch, value_branch, *gradients, *last, *results)
    key_grad, value_grad, filter_grad = results
    return (ungrouped(key_grad), ungrouped(value_grad), filter_grad)


def solution(mesh):
    in_specs = (
        P(("groups", "ctx"), None),
        P(("groups", "ctx"), None),
        P(("groups", "ctx"), None),
        P(("groups", "ctx"), None),
        P("ctx", None),
        P("groups"),
    )
    out_specs = (P(("groups", "ctx"), None), P(("groups", "ctx"), None), P(("groups", "ctx"), None))
    return jax.shard_map(shards, mesh=mesh, in_specs=in_specs, out_specs=out_specs, check_vma=False)
```
